32 devices in a mesh: batch: 4 (over x, core), ctx: 8 (over z, y).
Axes of the slice: x: 2, y: 2, z: 4, core: 2. Of those that a mesh axis runs over, the one named last changes fastest.
Arguments:
- event_rows: bfloat16 [4, 2048, 256], P('batch', 'ctx'), may hold values from -6 to 6
- event_index: int32 [4, 2048], P('batch', 'ctx'), may hold values from 0 to 16383, as said below
- decay: float32 [4, 16, 2048], P('batch', None, 'ctx'), may hold values from 0.15 to 1
- saved_state: float32 [4, 8, 16, 128, 64], P('batch', 'ctx'), may hold values from -6 to 6
- dout: bfloat16 [4, 2048, 512], P('batch', 'ctx'), may hold values from -0.29882812 to 0.29882812
- w_up: bfloat16 [256, 512], replicated, may hold values from -0.375 to 0.375
- w_in: bfloat16 [512, 1280], replicated, may hold values from -0.25 to 0.25
- w_out: bfloat16 [1024, 512], replicated, may hold values from -0.1875 to 0.1875
- skip: float32 [16], replicated, may hold values from 0.5 to 2
Outputs:
- grad_up: float32 [256, 512], replicated
- grad_in: float32 [512, 1280], replicated
- grad_out: float32 [1024, 512], replicated
- grad_skip: float32 [16], replicated
- grad_table: float32 [16384, 256], P(('batch', 'ctx'))
The draws below stay inside these ranges and needn't reach their ends.
Inputs may be any that keep to these rules, and one draw needn't show every extreme that they name: `event_index`: rows are in blocks of 512; block k is held by device k of batch+ctx. The 256 events of one device name rows of at most 16 events in any one block, and in every draw some block is named by exactly 16 events of every device.
All inputs are finite; a program needn't handle non-finite values.
Results may differ from the reference program's by a relative error of at most 0.011.
Values may be sent and summed in bfloat16 or wider, within the bound.
A program may use at most 128 MiB of HBM per device.

```python
from functools import partial
import jax
import jax.numpy as jnp
from jax import lax

D = 512
E = 256
HEADS = 16
HEAD = 64
STATE = 128
CH = 256
TOK_DEV = 256
ROWS_DEV = 512
INNER = 1024
PROJ = 1280
BATCH = 4
CTX_SHARDS = 8
SEQ = 2048
ROWS = 16384
CAP = 16
DEVICES = 32


def draw_decay(key, part):
    key_fast, key_rough, key_piece, key_spot, key_depth = jax.random.split(key, 5)
    is_fast = jax.random.randint(key_fast, (BATCH, HEADS, 1), 0, 2) == 0
    baseline_intensity = jnp.where(is_fast, 1.0 / 40.0, 0.3 / SEQ)
    coarse_estimate = jnp.exp(jax.random.uniform(key_rough, (BATCH, HEADS, SEQ), minval=-0.7, maxval=0.7))
    segment_multiplier = jnp.exp(jax.random.uniform(key_piece, (BATCH, HEADS, CTX_SHARDS, 1), minval=-0.7, maxval=0.7))
    segment_multiplier = jnp.broadcast_to(segment_multiplier, (BATCH, HEADS, CTX_SHARDS, TOK_DEV)).reshape(BATCH, HEADS, SEQ)
    marked_places = jax.random.randint(key_spot, (BATCH, 1, 3, 1), 0, SEQ)
    nesting_level = jax.random.uniform(key_depth, (BATCH, 1, 3, 1), minval=0.22, maxval=0.5)
    event_location = jnp.arange(SEQ, dtype=jnp.int32)[None, None, None, :]
    excitation_jump = jnp.sum(jnp.where(marked_places == event_location, nesting_level, 0.0), axis=2)
    return jnp.exp(-baseline_intensity * coarse_estimate * segment_multiplier - excitation_jump).astype(jnp.float32)


def draw_event_index(key, part):
    key_full, key_rank, key_score, key_order, key_row = jax.random.split(key, 5)
    owner_total = DEVICES
    full_owner = jax.random.randint(key_full, (), 0, owner_total)
    owner_rank = jax.random.permutation(key_rank, owner_total).astype(jnp.int32)
    owner_of_slot = jnp.repeat(jnp.arange(owner_total, dtype=jnp.int32), CAP)
    score = jax.random.randint(key_score, (BATCH, CTX_SHARDS, owner_total * CAP), 0, 65536) + owner_rank[owner_of_slot] * 1024
    score = jnp.where(owner_of_slot == full_owner, -1, score)
    chosen = jnp.argsort(score, axis=-1, stable=True)[..., :TOK_DEV]
    owners = owner_of_slot[chosen]
    order = jnp.argsort(jax.random.randint(key_order, (BATCH, CTX_SHARDS, TOK_DEV), 0, 1 << 30), axis=-1, stable=True)
    owners = jnp.take_along_axis(owners, order, axis=-1)
    local_row = jax.random.randint(key_row, (BATCH, CTX_SHARDS, TOK_DEV), 0, ROWS_DEV)
    return (owners * ROWS_DEV + local_row).reshape(BATCH, SEQ).astype(jnp.int32)


def shard_levels(own_key, extent, shards, low, high):
    level = 1.0
    for dim, shards_of in shards:
        steps = jax.random.uniform(jax.random.fold_in(jax.random.fold_in(own_key, 6), dim), (shards_of,), jnp.float32, low / len(shards), high / len(shards))
        level = level * jnp.repeat(jnp.exp(steps), extent[dim] // shards_of).reshape((-1,) + (1,) * (len(extent) - 1 - dim))
    return level


def gaussian(rng, shape, width, most, cuts=(), held_as=jnp.bfloat16):
    values = width * jax.random.normal(rng, shape, jnp.float32)
    if cuts:
        values = values * shard_levels(rng, shape, cuts, -0.22, 0.18)
    return jnp.clip(values, -most, most).astype(held_as)


def setup_inputs(seed: int = 0) -> dict:
    streams_of = jax.random.split(jax.random.key(seed), 10)
    return {
        "event_rows": gaussian(streams_of[0], (BATCH, SEQ, E), 1.0, 6.0, ((0, 4), (1, 8))),
        "event_index": draw_event_index(jax.random.fold_in(streams_of[9], 71), 0),
        "decay": draw_decay(jax.random.fold_in(streams_of[9], 71), 0),
        "saved_state": gaussian(streams_of[3], (BATCH, CTX_SHARDS, HEADS, STATE, HEAD), 1.0, 6.0, ((0, 4), (1, 8)), jnp.float32),
        "dout": gaussian(streams_of[4], (BATCH, SEQ, D), 0.05, 0.29882812, ((0, 4), (1, 8))),
        "w_up": gaussian(streams_of[5], (E, D), E ** -0.5, 0.375),
        "w_in": gaussian(streams_of[6], (D, PROJ), D ** -0.5, 0.25),
        "w_out": gaussian(streams_of[7], (INNER, D), INNER ** -0.5, 0.1875),
        "skip": jnp.clip(jax.random.uniform(streams_of[8], (HEADS,), jnp.float32, 0.5, 2.0), 0.5, 2.0),
    }


STEP_SIZE = 0.0625
exact_sum = partial(jnp.einsum, precision=lax.Precision.HIGHEST)


def block_parts(log_decay):
    cum_log = jnp.cumsum(log_decay, axis=1)
    length = log_decay.shape[1]
    causal = jnp.arange(length)[:, None] >= jnp.arange(length)[None, :]
    log_gap = cum_log[:, :, None] - cum_log[:, None, :]
    decay_mask = jnp.where(causal[None], jnp.exp(jnp.where(causal[None], log_gap, 0.0)), 0.0)
    return cum_log, decay_mask


def forward_block(h_start, x_part, b_part, c_part, log_decay, skip):
    state_scale = c_part.shape[1] ** -0.5
    cum_log, decay_mask = block_parts(log_decay)
    start_decay = jnp.exp(cum_log)
    c_dot_b = exact_sum("tn,sn->ts", c_part, b_part)
    within = STEP_SIZE * exact_sum("hts,ts,shp->thp", decay_mask, c_dot_b, x_part)
    from_start = exact_sum("tn,hnp->thp", c_part, h_start) * start_decay.T[:, :, None]
    y_out = state_scale * (from_start + within) + skip[None, :, None] * x_part
    tail_decay = jnp.exp(cum_log[:, -1:] - cum_log)
    h_end = jnp.exp(cum_log[:, -1])[:, None, None] * h_start + STEP_SIZE * exact_sum("hs,sn,shp->hnp", tail_decay, b_part, x_part)
    return y_out, h_end


def block_summary(c_part, dy_part, log_decay):
    state_scale = c_part.shape[1] ** -0.5
    cum_log = jnp.cumsum(log_decay, axis=1)
    amount = jnp.exp(cum_log[:, -1])
    block_sums = state_scale * exact_sum("ht,tn,thp->hnp", jnp.exp(cum_log), c_part, dy_part)
    return amount, block_sums


def backward_block(carry_in, h_start, x_part, b_part, c_part, dy_part, log_decay, skip):
    state_scale = c_part.shape[1] ** -0.5
    cum_log, decay_mask = block_parts(log_decay)
    start_decay = jnp.exp(cum_log)
    tail_decay = jnp.exp(cum_log[:, -1:] - cum_log)
    mask_back = jnp.swapaxes(decay_mask, 1, 2)
    b_dot_c = exact_sum("tn,sn->ts", b_part, c_part)
    x_dot_dy = exact_sum("thp,shp->hts", x_part, dy_part)
    dy_dot_x = jnp.swapaxes(x_dot_dy, 1, 2)
    dx_part = STEP_SIZE * (state_scale * exact_sum("hts,ts,shp->thp", mask_back, b_dot_c, dy_part)
                           + tail_decay.T[:, :, None] * exact_sum("tn,hnp->thp", b_part, carry_in)) + skip[None, :, None] * dy_part
    db_part = STEP_SIZE * (state_scale * exact_sum("hts,sn->tn", mask_back * x_dot_dy, c_part)
                           + exact_sum("ht,hnp,thp->tn", tail_decay, carry_in, x_part))
    dc_part = state_scale * (exact_sum("ht,hnp,thp->tn", start_decay, h_start, dy_part)
                             + STEP_SIZE * exact_sum("hts,sn->tn", decay_mask * dy_dot_x, b_part))
    dskip_part = exact_sum("thp,thp->h", x_part, dy_part)
    return dx_part, db_part, dc_part, dskip_part


def one_history(history_rows, history_index, history_decay, saved_blocks, history_dout, w_up, w_in, w_out, skip):
    length = history_rows.shape[0]
    inner_width = w_out.shape[0]
    head_count = skip.shape[0]
    head_size = inner_width // head_count
    state_width = (w_in.shape[1] - inner_width) // 2
    block_count = length // CH
    per_piece = TOK_DEV // CH
    u_rows = jnp.dot(history_rows, w_up, preferred_element_type=jnp.float32).astype(jnp.bfloat16)
    projected = jnp.dot(u_rows, w_in, preferred_element_type=jnp.float32).astype(jnp.bfloat16)
    dy_rows = jnp.dot(history_dout, w_out.T, preferred_element_type=jnp.float32).astype(jnp.bfloat16)
    x_all = projected[:, :inner_width].astype(jnp.float32).reshape(block_count, CH, head_count, head_size)
    b_all = projected[:, inner_width:inner_width + state_width].astype(jnp.float32).reshape(block_count, CH, state_width)
    c_all = projected[:, inner_width + state_width:].astype(jnp.float32).reshape(block_count, CH, state_width)
    dy_all = dy_rows.astype(jnp.float32).reshape(block_count, CH, head_count, head_size)
    log_all = jnp.log(history_decay).reshape(head_count, block_count, CH).transpose(1, 0, 2)

    def forward_step(h_state, block):
        x_part, b_part, c_part, log_decay, block_number = block
        saved_here = lax.dynamic_index_in_dim(saved_blocks, (block_number // per_piece).astype(jnp.int32), 0, keepdims=False)
        h_start = jnp.where(block_number % per_piece == 0, saved_here, h_state)
        y_out, h_end = forward_block(h_start, x_part, b_part, c_part, log_decay, skip)
        return h_end, (y_out, h_start)

    zero_state = jnp.zeros((head_count, state_width, head_size), jnp.float32)
    _, (y_blocks, starts) = lax.scan(forward_step, zero_state,
                                     (x_all, b_all, c_all, log_all, jnp.arange(block_count, dtype=jnp.int32)))
    y_rows = y_blocks.reshape(length, inner_width).astype(jnp.bfloat16)

    def backward_step(carried, block):
        h_start, x_part, b_part, c_part, dy_part, log_decay = block
        grads = backward_block(carried, h_start, x_part, b_part, c_part, dy_part, log_decay, skip)
        amount, block_sums = block_summary(c_part, dy_part, log_decay)
        return block_sums + amount[:, None, None] * carried, grads

    _, (dx_all, db_all, dc_all, dskip_all) = lax.scan(backward_step, zero_state,
                                                      (starts, x_all, b_all, c_all, dy_all, log_all), reverse=True)
    dprojected = jnp.concatenate([dx_all.reshape(length, inner_width), db_all.reshape(length, state_width),
                                  dc_all.reshape(length, state_width)], axis=1).astype(jnp.bfloat16)
    grad_out = jnp.dot(y_rows.T, history_dout, preferred_element_type=jnp.float32)
    grad_in = jnp.dot(u_rows.T, dprojected, preferred_element_type=jnp.float32)
    du_rows = jnp.dot(dprojected, w_in.T, preferred_element_type=jnp.float32).astype(jnp.bfloat16)
    grad_up = jnp.dot(history_rows.T, du_rows, preferred_element_type=jnp.float32)
    de_rows = jnp.dot(du_rows, w_up.T, preferred_element_type=jnp.float32).astype(jnp.bfloat16)
    grad_table = jax.ops.segment_sum(de_rows.astype(jnp.float32), history_index, num_segments=ROWS)
    return grad_up, grad_in, grad_out, jnp.sum(dskip_all, axis=0), grad_table


def reference(event_rows, event_index, decay, saved_state, dout, w_up, w_in, w_out, skip):
    def accumulate(totals, item):
        history_rows, history_index, history_decay, saved_blocks, history_dout = item
        parts = one_history(history_rows, history_index, history_decay, saved_blocks, history_dout, w_up, w_in, w_out, skip)
        return tuple(total + part for total, part in zip(totals, parts)), None

    initial = (jnp.zeros(w_up.shape, jnp.float32), jnp.zeros(w_in.shape, jnp.float32),
               jnp.zeros(w_out.shape, jnp.float32), jnp.zeros(skip.shape, jnp.float32),
               jnp.zeros((ROWS, event_rows.shape[2]), jnp.float32))
    totals, _ = lax.scan(accumulate, initial, (event_rows, event_index, decay, saved_state, dout))
    return totals[0], totals[1], totals[2], totals[3], totals[4]
```

```python
from functools import partial

import jax
import jax.numpy as jnp
from jax import lax
from jax.experimental import pallas as pl
from jax.experimental.pallas import tpu as pltpu
from jax.sharding import PartitionSpec as P

ROWS_DEV = 512
ROWS_BITS = 9
STEP_SIZE = 0.0625
LANES = 128
TILE = 16
MESH = pl.DeviceIdType.MESH
F32 = jnp.float32
BF16 = jnp.bfloat16
VMEM = pl.BlockSpec(memory_space=pltpu.VMEM)
SMEM = pl.BlockSpec(memory_space=pltpu.SMEM)
LIMIT = 48 * 1024 * 1024


def mm(a, b):
    return lax.dot_general(a, b, (((1,), (0,)), ((), ())), preferred_element_type=F32)


def mm_t(a, b):
    return lax.dot_general(a, b, (((1,), (1,)), ((), ())), preferred_element_type=F32)


def t_mm(a, b):
    return lax.dot_general(a, b, (((0,), (0,)), ((), ())), preferred_element_type=F32)


def exact_mm_t(a, b):
    return lax.dot_general(
        a, b, (((1,), (1,)), ((), ())), precision=lax.Precision.HIGHEST, preferred_element_type=F32
    )


def cut(j):
    return slice(LANES * j, LANES * (j + 1))


def front(er, decay, hs, dout, w_up, w_in, w_out, skip,
          u_out, x_out, b_out, dxl_out, tail_out, db_out, dc_out, sums_out, amount_out, dsk_out, gout_out,
          y_buf):
    tokens = er.shape[0]
    inner = w_out.shape[0]
    state = b_out.shape[1]
    heads = decay.shape[0]
    scale = state ** -0.5
    u = mm(er[...], w_up[...]).astype(BF16)
    u_out[...] = u
    proj = mm(u, w_in[...]).astype(BF16)
    x_out[...] = proj[:, :inner]
    b = proj[:, inner:inner + state]
    c = proj[:, inner + state:]
    b_out[...] = b
    dy = mm_t(dout[...], w_out[...]).astype(BF16)
    logs = jnp.log(decay[...])
    rows = lax.broadcasted_iota(jnp.int32, (tokens, tokens), 0)
    cols = lax.broadcasted_iota(jnp.int32, (tokens, tokens), 1)
    causal = rows >= cols
    tri = jnp.where(causal, 1.0, 0.0).astype(F32)
    cum_col = exact_mm_t(tri, logs)
    cum_row = exact_mm_t(logs, tri)
    total = cum_col[tokens - 1:tokens, :]
    start = jnp.exp(cum_col)
    tail = jnp.exp(total - cum_col)
    amount = jnp.exp(total)
    cb = jnp.where(causal, mm_t(c, b), 0.0)
    first = lax.broadcasted_iota(jnp.int32, (1, LANES), 1) < LANES // 2
    weight = jnp.zeros((tokens, tokens), F32)
    dc = jnp.zeros((tokens, state), F32)
    for j in range(heads // 2):
        xp = proj[:, cut(j)]
        dyp = dy[:, cut(j)]
        xf = xp.astype(F32)
        dyf = dyp.astype(F32)
        forward, backward = [], []
        prod = jnp.sum(xf * dyf, axis=0, keepdims=True)
        for i in range(2):
            h = 2 * j + i
            mine = first if i == 0 else jnp.logical_not(first)
            mask = jnp.exp(jnp.minimum(cum_col[:, h:h + 1] - cum_row[h:h + 1, :], 0.0))
            g = (mask * cb).astype(BF16)
            forward.append(mm(g, xp))
            backward.append(t_mm(g, dyp))
            weight += mask * mm_t(jnp.where(mine, dyf, 0.0).astype(BF16), xp)
            dsk_out[h:h + 1, :] = jnp.broadcast_to(
                jnp.sum(jnp.where(mine, prod, 0.0), axis=1, keepdims=True), (1, LANES))

        def spread(a):
            return jnp.where(first, a[:, 2 * j:2 * j + 1], a[:, 2 * j + 1:2 * j + 2])

        start_p = spread(start)
        skip_p = jnp.where(first, skip[2 * j], skip[2 * j + 1])
        hs_p = jnp.concatenate([hs[2 * j], hs[2 * j + 1]], axis=1).astype(BF16)
        within = jnp.where(first, forward[0], forward[1])
        y = scale * (mm(c, hs_p) * start_p + STEP_SIZE * within) + skip_p * xf
        y_buf[:, cut(j)] = y.astype(BF16)
        dxl_out[:, cut(j)] = (STEP_SIZE * scale) * jnp.where(first, backward[0], backward[1]) + skip_p * dyf
        tail_out[:, cut(j)] = spread(tail)
        sdy = (start_p * dyf).astype(BF16)
        half, k = j // (heads // 4), j % (heads // 4)
        sums_out[half, :, cut(k)] = (scale * t_mm(c, sdy)).astype(BF16)
        amount_out[half, :, cut(k)] = jnp.broadcast_to(spread(amount), (8, LANES))
        dc += mm_t(sdy, hs_p)
    weight = jnp.where(causal, weight, 0.0).astype(BF16)
    dc_out[...] = scale * (dc + STEP_SIZE * mm(weight, b))
    db_out[...] = (STEP_SIZE * scale) * t_mm(weight, c)
    y_all = y_buf[...]
    for j in range(dout.shape[1] // LANES):
        gout_out[inner * j:inner * (j + 1), :] = t_mm(y_all, dout[:, cut(j)]).astype(BF16)


def back(cap, er, idx_row, idx_col, u, x, b, dxl, tail, db, dc, dsk, carry, w_up, w_in,
         grads_out, send_out):
    tokens = er.shape[0]
    inner = x.shape[1]
    half = inner // 2
    carry_all = jnp.concatenate([carry[0], carry[1]], axis=1)
    tail_v = tail[...]
    dx = dxl[...] + STEP_SIZE * tail_v * mm(b[...], carry_all)
    dbv = db[...] + STEP_SIZE * mm_t((tail_v * x[...].astype(F32)).astype(BF16), carry_all)
    dproj = jnp.concatenate([dx.astype(BF16), dbv.astype(BF16), dc[...].astype(BF16)], axis=1)
    du = mm_t(dproj, w_in[...]).astype(BF16)
    de = mm_t(du, w_up[...]).astype(BF16)
    owner_row = lax.shift_right_logical(idx_row[...], ROWS_BITS)
    owner_col = lax.shift_right_logical(idx_col[...], ROWS_BITS)
    earlier = lax.broadcasted_iota(jnp.int32, (tokens, tokens), 0) < lax.broadcasted_iota(
        jnp.int32, (tokens, tokens), 1)
    rank = jnp.sum(
        jnp.where(jnp.logical_and(earlier, owner_col == owner_row), 1.0, 0.0), axis=0, keepdims=True)
    slot = owner_row * cap + rank.astype(jnp.int32)
    slots = send_out.shape[0]
    pick = jnp.where(
        lax.broadcasted_iota(jnp.int32, (slots, tokens), 0) == slot, 1.0, 0.0).astype(BF16)
    number = idx_col[...] - owner_col * ROWS_DEV + 1
    high = lax.shift_right_logical(number, 8)
    low = number - high * 256
    lane = lax.broadcasted_iota(jnp.int32, (tokens, LANES), 1)
    tags = jnp.where(lane == 0, high.astype(F32), jnp.where(lane == 1, low.astype(F32), 0.0))
    width = de.shape[1]
    send_out[:, :width] = mm(pick, de).astype(BF16)
    value = dsk[...]
    one = value.astype(BF16).astype(F32)
    two = (value - one).astype(BF16).astype(F32)
    three = value - one - two
    place = lax.broadcasted_iota(jnp.int32, value.shape, 1)
    share = jnp.where(place == 2, one, jnp.where(place == 3, two, jnp.where(place == 4, three, 0.0)))
    if cap > share.shape[0]:
        share = jnp.concatenate([share, jnp.zeros((cap - share.shape[0], LANES), F32)], axis=0)
    tagged = mm(pick, tags.astype(BF16)).reshape(slots // cap, cap, LANES) + share[None]
    send_out[:, width:] = tagged.reshape(slots, LANES).astype(BF16)
    erv = er[...]
    for j in range(du.shape[1] // LANES):
        grads_out[width * j:width * (j + 1), :] = t_mm(erv, du[:, cut(j)]).astype(BF16)
    base = width * (du.shape[1] // LANES)
    uv = u[...]
    depth = uv.shape[1]
    for j in range(dproj.shape[1] // LANES):
        grads_out[base + depth * j:base + depth * (j + 1), :] = t_mm(uv, dproj[:, cut(j)]).astype(BF16)


def unpack(gout, grads, arrived, grad_up, grad_in, grad_out, grad_skip, grad_table):
    inner = grad_out.shape[0]
    for j in range(grad_out.shape[1] // LANES):
        grad_out[:, cut(j)] = gout[inner * j:inner * (j + 1), :].astype(F32)
    width, depth = grad_up.shape
    for j in range(depth // LANES):
        grad_up[:, cut(j)] = grads[width * j:width * (j + 1), :].astype(F32)
    base = width * (depth // LANES)
    for j in range(grad_in.shape[1] // LANES):
        grad_in[:, cut(j)] = grads[base + depth * j:base + depth * (j + 1), :].astype(F32)
    tags = arrived[:, width:].astype(F32)
    number = tags[:, 0:1] * 256.0 + tags[:, 1:2] - 1.0
    slots = tags.shape[0]
    row = lax.broadcasted_iota(jnp.int32, (slots, ROWS_DEV), 1).astype(F32)
    pick = jnp.where(row == number, 1.0, 0.0).astype(BF16)
    grad_table[...] = t_mm(pick, arrived[:, :width])
    heads = grad_skip.shape[0]
    cap = TILE
    parts = jnp.sum(tags.reshape(slots // cap, cap, LANES), axis=0)[:heads]
    place = lax.broadcasted_iota(jnp.int32, parts.shape, 1)
    kept = jnp.where(jnp.logical_and(place >= 2, place <= 4), parts, 0.0)
    grad_skip[...] = jnp.broadcast_to(jnp.sum(kept, axis=1, keepdims=True), grad_skip.shape)


def bit_count(n):
    return n.bit_length() - 1


class Summing:
    def __init__(self, rows, batch_n, ctx_n):
        self.names = [("batch", i) for i in range(bit_count(batch_n))]
        self.names += [("ctx", i) for i in range(bit_count(ctx_n))]
        self.levels = len(self.names)
        tiles = rows // (batch_n * ctx_n) // TILE
        self.streams = []
        base = 0
        recv = 0
        rest = self.names[1:]
        for s in range(3):
            mine = (tiles + 2 - s) // 3
            if mine == 0:
                continue
            turn = rest[:3]
            order = self.names[:1] + turn[s:] + turn[:s] + rest[3:]
            size = mine * TILE << self.levels
            slots = []
            for k in range(self.levels):
                slots.append(recv)
                recv += size >> (k + 1)
            self.streams.append((base, size, order, slots))
            base += size
        self.recv_rows = recv
        self.sems = len(self.streams) * self.levels * 2

    def scratch(self, rows):
        return [
            pltpu.VMEM((rows, LANES), BF16),
            pltpu.VMEM((self.recv_rows, LANES), BF16),
            pltpu.VMEM((rows, LANES), BF16),
            pltpu.SemaphoreType.DMA((self.sems,)),
            pltpu.SemaphoreType.DMA((self.sems,)),
        ]

    def partners(self, where):
        out = []
        for axis, bit in self.names:
            out.append(self.partner(where, axis, bit)[0])
        return out

    def partner(self, where, axis, bit):
        at = where[axis]
        mine = (at // (1 << bit)) % 2
        other = at + (1 - 2 * mine) * (1 << bit)
        target = (other, where["ctx"]) if axis == "batch" else (where["batch"], other)
        return target, mine

    def bind(self, where, acc, recv, full, send_sem, recv_sem):
        self.acc, self.recv, self.full = acc, recv, full
        self.copies = []
        self.keeps = []
        for s, (base, size, order, slots) in enumerate(self.streams):
            off = base
            down, up, keeps = [], [], []
            for k, (axis, bit) in enumerate(order):
                target, mine = self.partner(where, axis, bit)
                half = size >> (k + 1)
                keep = pl.multiple_of(off + mine * half, TILE)
                away = pl.multiple_of(off + (1 - mine) * half, TILE)
                n = (s * self.levels + k) * 2
                down.append(pltpu.make_async_remote_copy(
                    src_ref=acc.at[pl.ds(away, half)], dst_ref=recv.at[pl.ds(slots[k], half)],
                    send_sem=send_sem.at[n], recv_sem=recv_sem.at[n],
                    device_id=target, device_id_type=MESH))
                up.append(pltpu.make_async_remote_copy(
                    src_ref=full.at[pl.ds(keep, half)], dst_ref=full.at[pl.ds(keep, half)],
                    send_sem=send_sem.at[n + 1], recv_sem=recv_sem.at[n + 1],
                    device_id=target, device_id_type=MESH))
                keeps.append((keep, half, slots[k]))
                off = keep
            self.copies.append((down, up))
            self.keeps.append(keeps)

    def begin(self):
        for down, _ in self.copies:
            down[0].start()

    def step(self, k):
        last = self.levels - 1
        for s, (down, up) in enumerate(self.copies):
            if k <= last:
                down[k].wait()
                keep, half, slot = self.keeps[s][k]
                total = self.acc[pl.ds(keep, half), :].astype(F32) + self.recv[pl.ds(slot, half), :].astype(F32)
                if k < last:
                    self.acc[pl.ds(keep, half), :] = total.astype(BF16)
                    down[k + 1].start()
                else:
                    self.full[pl.ds(keep, half), :] = total.astype(BF16)
                    up[last].start()
            else:
                n = 2 * self.levels - 1 - k
                up[n].wait()
                if n > 0:
                    up[n - 1].start()

    @property
    def steps(self):
        return 2 * self.levels


def position():
    return {"batch": lax.axis_index("batch"), "ctx": lax.axis_index("ctx")}


def carry_kernel(summing, ctx_n, sums, amount, gout, carry_out, gout_out,
                 acc, recv, full, send_sem, recv_sem,
                 other, other_amount, moving, entering, entering_other, c_send, c_recv):
    where = position()
    batch, ctx = where["batch"], where["ctx"]
    pair, place = ctx // 2, ctx % 2
    pairs = ctx_n // 2
    acc[...] = gout[...]
    entering[...] = jnp.zeros_like(entering)
    partner = (batch, ctx + 1 - 2 * place)
    earlier = (batch, jnp.maximum(ctx - 2, 0))

    barrier = pltpu.get_barrier_semaphore()
    targets = summing.partners(where)
    for target in targets:
        pl.semaphore_signal(barrier, inc=1, device_id=target, device_id_type=MESH)

    for near in ((ctx + 2) % ctx_n, (ctx + ctx_n - 2) % ctx_n):
        pl.semaphore_signal(barrier, inc=1, device_id=(batch, near), device_id_type=MESH)
    pl.semaphore_wait(barrier, len(targets) + 2)

    def send(src, dst, n, target):
        return pltpu.make_async_remote_copy(
            src_ref=src, dst_ref=dst, send_sem=c_send.at[n], recv_sem=c_recv.at[n],
            device_id=target, device_id_type=MESH)

    amounts = send(amount, other_amount, 0, partner)
    halves = send(sums.at[1 - place], other.at[1 - place], 1, partner)
    second = send(sums.at[1], other.at[1], 2, partner)
    hop = send(moving, entering, 3, earlier)
    cross = send(entering, entering_other, 4, partner)
    amounts.start()
    halves.start()

    @pl.when(place == 1)
    def _():
        second.start()

    summing.bind(where, acc, recv, full, send_sem, recv_sem)
    summing.begin()
    amounts.wait()
    halves.wait()
    mine = sums[place].astype(F32)
    theirs = other[place].astype(F32)
    a_mine = amount[place][0:1]
    a_theirs = other_amount[place][0:1]
    is_first = place == 0
    whole = jnp.where(is_first, mine + a_mine * theirs, theirs + a_theirs * mine)
    a_whole = a_mine * a_theirs
    done = 0
    for h in range(pairs - 2, -1, -1):
        @pl.when(pair == h + 1)
        def _():
            moving[...] = (whole + a_whole * entering[...].astype(F32)).astype(BF16)
            hop.start()

        @pl.when(pair == h)
        def _():
            hop.wait_recv()

        if done < summing.levels:
            summing.step(done)
            done += 1
    cross.start()
    if done < summing.steps:
        summing.step(done)
        done += 1
    cross.wait()

    @pl.when(place == 1)
    def _():
        second.wait_send()
        carry_out[1] = entering[...]
        carry_out[0] = entering_other[...]

    @pl.when(place == 0)
    def _():
        second.wait_recv()
        carry_out[0] = (other[0].astype(F32) + other_amount[0][0:1] * entering[...].astype(F32)).astype(BF16)
        carry_out[1] = (other[1].astype(F32) + other_amount[1][0:1] * entering_other[...].astype(F32)).astype(BF16)

    @pl.when(pair > 0)
    def _():
        hop.wait_send()

    while done < summing.steps:
        summing.step(done)
        done += 1
    gout_out[...] = full[...]


def final_kernel(summing, cap, batch_n, ctx_n, grads, rows, grads_out, arrived_out,
                 acc, recv, full, send_sem, recv_sem, arrived, r_send, r_recv, own_sem):
    where = position()
    batch, ctx = where["batch"], where["ctx"]
    me = batch * ctx_n + ctx
    count = batch_n * ctx_n
    acc[...] = grads[...]
    barrier = pltpu.get_barrier_semaphore()

    def at(step):
        to = (me + step) % count
        return to, (to // ctx_n, to % ctx_n)

    def hello(step, _):
        pl.semaphore_signal(barrier, inc=1, device_id=at(step)[1], device_id_type=MESH)
        return 0

    lax.fori_loop(1, count, hello, 0)
    pl.semaphore_wait(barrier, count - 1)
    summing.bind(where, acc, recv, full, send_sem, recv_sem)
    summing.begin()
    mine = pl.ds(pl.multiple_of(me * cap, TILE), cap)
    own = pltpu.make_async_copy(rows.at[mine], arrived.at[mine], own_sem)
    own.start()

    def row_copy(step):
        to, target = at(step)
        return pltpu.make_async_remote_copy(
            src_ref=rows.at[pl.ds(pl.multiple_of(to * cap, TILE), cap)], dst_ref=arrived.at[mine],
            send_sem=r_send.at[step], recv_sem=r_recv.at[step],
            device_id=target, device_id_type=MESH)

    def launch(step, _):
        row_copy(step).start()
        return 0

    lax.fori_loop(1, count, launch, 0)
    for k in range(summing.steps):
        summing.step(k)

    def finish(step, _):
        row_copy(step).wait()
        return 0

    lax.fori_loop(1, count, finish, 0)
    own.wait()
    grads_out[...] = full[...]
    arrived_out[...] = arrived[...]


def local(event_rows, event_index, decay, saved_state, dout, w_up, w_in, w_out, skip):
    batch_n = lax.axis_size("batch")
    ctx_n = lax.axis_size("ctx")
    count = batch_n * ctx_n
    er = event_rows[0]
    tokens, width = er.shape
    inner, depth = w_out.shape
    proj = w_in.shape[1]
    state = (proj - inner) // 2
    heads = skip.shape[0]
    half = inner // 2
    cap = TILE
    shape = jax.ShapeDtypeStruct
    params = pltpu.CompilerParams(vmem_limit_bytes=LIMIT)
    gout_rows = inner * depth // LANES
    grad_rows = (width * depth + depth * proj) // LANES
    u, x, b, dxl, tail, db, dc, sums, amount, dsk, gout = pl.pallas_call(
        front,
        out_shape=(
            shape((tokens, depth), BF16), shape((tokens, inner), BF16), shape((tokens, state), BF16),
            shape((tokens, inner), F32), shape((tokens, inner), F32), shape((tokens, state), F32),
            shape((tokens, state), F32), shape((2, state, half), BF16), shape((2, 8, half), F32),
            shape((heads, LANES), F32), shape((gout_rows, LANES), BF16),
        ),
        in_specs=[VMEM] * 7 + [SMEM],
        out_specs=[VMEM] * 11,
        scratch_shapes=[pltpu.VMEM((tokens, inner), BF16)],
        compiler_params=params,
        name="front",
    )(er, decay[0], saved_state[0, 0], dout[0], w_up, w_in, w_out, skip)

    summing = Summing(gout_rows, batch_n, ctx_n)
    carry, gout = pl.pallas_call(
        partial(carry_kernel, summing, ctx_n),
        out_shape=(shape((2, state, half), BF16), shape((gout_rows, LANES), BF16)),
        in_specs=[VMEM] * 3,
        out_specs=[VMEM] * 2,
        scratch_shapes=summing.scratch(gout_rows) + [
            pltpu.VMEM((2, state, half), BF16),
            pltpu.VMEM((2, 8, half), F32),
            pltpu.VMEM((state, half), BF16),
            pltpu.VMEM((state, half), BF16),
            pltpu.VMEM((state, half), BF16),
            pltpu.SemaphoreType.DMA((5,)),
            pltpu.SemaphoreType.DMA((5,)),
        ],
        compiler_params=pltpu.CompilerParams(
            vmem_limit_bytes=LIMIT, collective_id=0, has_side_effects=True),
        name="carry",
    )(sums, amount, gout)

    grads, rows = pl.pallas_call(
        partial(back, cap),
        out_shape=(shape((grad_rows, LANES), BF16), shape((count * cap, width + LANES), BF16)),
        in_specs=[VMEM] * 14,
        out_specs=[VMEM] * 2,
        compiler_params=params,
        name="back",
    )(er, event_index, event_index.reshape(tokens, 1), u, x, b, dxl, tail, db, dc, dsk, carry, w_up, w_in)

    summing = Summing(grad_rows, batch_n, ctx_n)
    grads, arrived = pl.pallas_call(
        partial(final_kernel, summing, cap, batch_n, ctx_n),
        out_shape=(shape(grads.shape, BF16), shape(rows.shape, BF16)),
        in_specs=[VMEM] * 2,
        out_specs=[VMEM] * 2,
        scratch_shapes=summing.scratch(grad_rows) + [
            pltpu.VMEM(rows.shape, BF16),
            pltpu.SemaphoreType.DMA((count,)),
            pltpu.SemaphoreType.DMA((count,)),
            pltpu.SemaphoreType.DMA,
        ],
        compiler_params=pltpu.CompilerParams(
            vmem_limit_bytes=LIMIT, collective_id=1, has_side_effects=True),
        name="final",
    )(grads, rows)

    grad_up, grad_in, grad_out, grad_skip, grad_table = pl.pallas_call(
        unpack,
        out_shape=(
            shape((width, depth), F32), shape((depth, proj), F32), shape((inner, depth), F32),
            shape((heads, LANES), F32), shape((ROWS_DEV, width), F32),
        ),
        in_specs=[VMEM] * 3,
        out_specs=[VMEM] * 5,
        compiler_params=params,
        name="unpack",
    )(gout, grads, arrived)
    return grad_up, grad_in, grad_out, grad_skip[:, 0], grad_table


def solution(mesh):
    in_specs = (
        P("batch", "ctx", None),
        P("batch", "ctx"),
        P("batch", None, "ctx"),
        P("batch", "ctx", None, None, None),
        P("batch", "ctx", None),
        P(),
        P(),
        P(),
        P(),
    )
    out_specs = (P(), P(), P(), P(), P(("batch", "ctx"), None))
    return jax.shard_map(local, mesh=mesh, in_specs=in_specs, out_specs=out_specs, check_vma=False)
```

```python
from functools import partial

import jax
import jax.numpy as jnp
from jax import lax
from jax.experimental import pallas as pl
from jax.experimental.pallas import tpu as pltpu
from jax.sharding import PartitionSpec as P

ROWS_DEV = 512
ROWS_BITS = 9
STEP_SIZE = 0.0625
LANES = 128
TILE = 16
MESH = pl.DeviceIdType.MESH
F32 = jnp.float32
BF16 = jnp.bfloat16
VMEM = pl.BlockSpec(memory_space=pltpu.VMEM)
SMEM = pl.BlockSpec(memory_space=pltpu.SMEM)
LIMIT = 48 * 1024 * 1024


def mm(a, b):
    return lax.dot_general(a, b, (((1,), (0,)), ((), ())), preferred_element_type=F32)


def mm_t(a, b):
    return lax.dot_general(a, b, (((1,), (1,)), ((), ())), preferred_element_type=F32)


def t_mm(a, b):
    return lax.dot_general(a, b, (((0,), (0,)), ((), ())), preferred_element_type=F32)


def exact_mm_t(a, b):
    return lax.dot_general(
        a, b, (((1,), (1,)), ((), ())), precision=lax.Precision.HIGHEST, preferred_element_type=F32
    )


def cut(j):
    return slice(LANES * j, LANES * (j + 1))


def front(cap, er, idx, decay, hs, dout, w_up, w_in, w_out, skip,
          u_out, x_out, b_out, dxl_out, tail_out, db_out, dc_out, sums_out, amount_out, gout_out,
          pick_out, tags_out, y_buf, dsk):
    tokens = er.shape[0]
    inner = w_out.shape[0]
    state = b_out.shape[1]
    heads = decay.shape[0]
    scale = state ** -0.5
    u = mm(er[...], w_up[...]).astype(BF16)
    u_out[...] = u
    proj = mm(u, w_in[...]).astype(BF16)
    x_out[...] = proj[:, :inner]
    b = proj[:, inner:inner + state]
    c = proj[:, inner + state:]
    b_out[...] = b
    dy = mm_t(dout[...], w_out[...]).astype(BF16)
    logs = jnp.log(decay[...])
    rows = lax.broadcasted_iota(jnp.int32, (tokens, tokens), 0)
    cols = lax.broadcasted_iota(jnp.int32, (tokens, tokens), 1)
    causal = rows >= cols
    tri = jnp.where(causal, 1.0, 0.0).astype(F32)
    cum_col = exact_mm_t(tri, logs)
    cum_row = exact_mm_t(logs, tri)
    total = cum_col[tokens - 1:tokens, :]
    start = jnp.exp(cum_col)
    tail = jnp.exp(total - cum_col)
    amount = jnp.exp(total)
    cb = jnp.where(causal, mm_t(c, b), 0.0)
    first = lax.broadcasted_iota(jnp.int32, (1, LANES), 1) < LANES // 2
    weight = jnp.zeros((tokens, tokens), F32)
    dc = jnp.zeros((tokens, state), F32)
    for j in range(heads // 2):
        xp = proj[:, cut(j)]
        dyp = dy[:, cut(j)]
        xf = xp.astype(F32)
        dyf = dyp.astype(F32)
        forward, backward = [], []
        prod = jnp.sum(xf * dyf, axis=0, keepdims=True)
        for i in range(2):
            h = 2 * j + i
            mine = first if i == 0 else jnp.logical_not(first)
            mask = jnp.exp(jnp.minimum(cum_col[:, h:h + 1] - cum_row[h:h + 1, :], 0.0))
            g = (mask * cb).astype(BF16)
            forward.append(mm(g, xp))
            backward.append(t_mm(g, dyp))
            weight += mask * mm_t(jnp.where(mine, dyf, 0.0).astype(BF16), xp)
            dsk[h:h + 1, :] = jnp.broadcast_to(
                jnp.sum(jnp.where(mine, prod, 0.0), axis=1, keepdims=True), (1, LANES))

        def spread(a):
            return jnp.where(first, a[:, 2 * j:2 * j + 1], a[:, 2 * j + 1:2 * j + 2])

        start_p = spread(start)
        skip_p = jnp.where(first, skip[2 * j], skip[2 * j + 1])
        hs_p = hs[LANES * j:LANES * (j + 1), :].astype(BF16)
        within = jnp.where(first, forward[0], forward[1])
        y = scale * (mm_t(c, hs_p) * start_p + STEP_SIZE * within) + skip_p * xf
        y_buf[:, cut(j)] = y.astype(BF16)
        dxl_out[:, cut(j)] = (STEP_SIZE * scale) * jnp.where(first, backward[0], backward[1]) + skip_p * dyf
        tail_out[:, cut(j)] = spread(tail)
        sdy = (start_p * dyf).astype(BF16)
        half, k = j // (heads // 4), j % (heads // 4)
        sums_out[half, :, cut(k)] = (scale * t_mm(c, sdy)).astype(BF16)
        amount_out[half, :, cut(k)] = jnp.broadcast_to(spread(amount), (8, LANES))
        dc += mm(sdy, hs_p)
    weight = jnp.where(causal, weight, 0.0).astype(BF16)
    dc_out[...] = scale * (dc + STEP_SIZE * mm(weight, b))
    db_out[...] = (STEP_SIZE * scale) * t_mm(weight, c)
    y_all = y_buf[...]
    for j in range(dout.shape[1] // LANES):
        gout_out[inner * j:inner * (j + 1), :] = t_mm(y_all, dout[:, cut(j)]).astype(BF16)
    route(cap, idx[...], dsk[...], pick_out, tags_out)


def route(cap, idx_row, value, pick_out, tags_out):
    slots, tokens = pick_out.shape
    spread = jnp.broadcast_to(idx_row.astype(F32), (LANES, tokens))
    idx_col = spread.T[:, 0:1].astype(jnp.int32)
    owner_row = lax.shift_right_logical(idx_row, ROWS_BITS)
    owner_col = lax.shift_right_logical(idx_col, ROWS_BITS)
    earlier = lax.broadcasted_iota(jnp.int32, (tokens, tokens), 0) < lax.broadcasted_iota(
        jnp.int32, (tokens, tokens), 1)
    rank = jnp.sum(
        jnp.where(jnp.logical_and(earlier, owner_col == owner_row), 1.0, 0.0), axis=0, keepdims=True)
    slot = owner_row * cap + rank.astype(jnp.int32)
    pick = jnp.where(
        lax.broadcasted_iota(jnp.int32, (slots, tokens), 0) == slot, 1.0, 0.0).astype(BF16)
    pick_out[...] = pick
    number = idx_col - owner_col * ROWS_DEV + 1
    high = lax.shift_right_logical(number, 8)
    low = number - high * 256
    lane = lax.broadcasted_iota(jnp.int32, (tokens, LANES), 1)
    tags = jnp.where(lane == 0, high.astype(F32), jnp.where(lane == 1, low.astype(F32), 0.0))
    one = value.astype(BF16).astype(F32)
    two = (value - one).astype(BF16).astype(F32)
    three = value - one - two
    place = lax.broadcasted_iota(jnp.int32, value.shape, 1)
    share = jnp.where(place == 2, one, jnp.where(place == 3, two, jnp.where(place == 4, three, 0.0)))
    if cap > share.shape[0]:
        share = jnp.concatenate([share, jnp.zeros((cap - share.shape[0], LANES), F32)], axis=0)
    tagged = mm(pick, tags.astype(BF16)).reshape(slots // cap, cap, LANES) + share[None]
    tags_out[...] = tagged.reshape(slots, LANES).astype(BF16)


def back(er, u, x, b, dxl, tail, db, dc, carry, w_in, grads_out):
    carry_all = jnp.concatenate([carry[0], carry[1]], axis=1)
    tail_v = tail[...]
    dx = dxl[...] + STEP_SIZE * tail_v * mm(b[...], carry_all)
    dbv = db[...] + STEP_SIZE * mm_t((tail_v * x[...].astype(F32)).astype(BF16), carry_all)
    dproj = jnp.concatenate([dx.astype(BF16), dbv.astype(BF16), dc[...].astype(BF16)], axis=1)
    du = mm_t(dproj, w_in[...]).astype(BF16)
    erv = er[...]
    width = erv.shape[1]
    for j in range(du.shape[1] // LANES):
        grads_out[width * j:width * (j + 1), :] = t_mm(erv, du[:, cut(j)]).astype(BF16)
    base = width * (du.shape[1] // LANES)
    uv = u[...]
    depth = uv.shape[1]
    for j in range(dproj.shape[1] // LANES):
        grads_out[base + depth * j:base + depth * (j + 1), :] = t_mm(uv, dproj[:, cut(j)]).astype(BF16)
    return du


def unpack(gout, grads, arrived, grad_up, grad_in, grad_out, grad_skip, grad_table):
    inner = grad_out.shape[0]
    for j in range(grad_out.shape[1] // LANES):
        grad_out[:, cut(j)] = gout[inner * j:inner * (j + 1), :].astype(F32)
    width, depth = grad_up.shape
    for j in range(depth // LANES):
        grad_up[:, cut(j)] = grads[width * j:width * (j + 1), :].astype(F32)
    base = width * (depth // LANES)
    for j in range(grad_in.shape[1] // LANES):
        grad_in[:, cut(j)] = grads[base + depth * j:base + depth * (j + 1), :].astype(F32)
    tags = arrived[:, width:].astype(F32)
    number = tags[:, 0:1] * 256.0 + tags[:, 1:2] - 1.0
    slots = tags.shape[0]
    row = lax.broadcasted_iota(jnp.int32, (slots, ROWS_DEV), 1).astype(F32)
    pick = jnp.where(row == number, 1.0, 0.0).astype(BF16)
    grad_table[...] = t_mm(pick, arrived[:, :width])
    heads = grad_skip.shape[1]
    cap = TILE
    parts = jnp.sum(tags.reshape(slots // cap, cap, LANES), axis=0)[:heads]
    place = lax.broadcasted_iota(jnp.int32, parts.shape, 1)
    kept = jnp.where(jnp.logical_and(place >= 2, place <= 4), parts, 0.0)
    sums = jnp.sum(kept, axis=1, keepdims=True)
    same = lax.broadcasted_iota(jnp.int32, (heads, heads), 0) == lax.broadcasted_iota(
        jnp.int32, (heads, heads), 1)
    grad_skip[...] = jnp.sum(jnp.where(same, sums, 0.0), axis=0, keepdims=True)


def bit_count(n):
    return n.bit_length() - 1


class Summing:
    def __init__(self, rows, batch_n, ctx_n):
        self.names = [("batch", i) for i in range(bit_count(batch_n))]
        self.names += [("ctx", i) for i in range(bit_count(ctx_n))]
        self.levels = len(self.names)
        tiles = rows // (batch_n * ctx_n) // TILE
        self.streams = []
        base = 0
        recv = 0
        rest = self.names[1:]
        for s in range(3):
            mine = (tiles + 2 - s) // 3
            if mine == 0:
                continue
            turn = rest[:3]
            order = self.names[:1] + turn[s:] + turn[:s] + rest[3:]
            size = mine * TILE << self.levels
            slots = []
            for k in range(self.levels):
                slots.append(recv)
                recv += size >> (k + 1)
            self.streams.append((base, size, order, slots))
            base += size
        self.recv_rows = recv
        self.sems = len(self.streams) * self.levels * 2

    def scratch(self, rows):
        return [
            pltpu.VMEM((rows, LANES), BF16),
            pltpu.VMEM((self.recv_rows, LANES), BF16),
            pltpu.VMEM((rows, LANES), BF16),
            pltpu.SemaphoreType.DMA((self.sems,)),
            pltpu.SemaphoreType.DMA((self.sems,)),
        ]

    def partners(self, where):
        out = []
        for axis, bit in self.names:
            out.append(self.partner(where, axis, bit)[0])
        return out

    def partner(self, where, axis, bit):
        at = where[axis]
        mine = (at // (1 << bit)) % 2
        other = at + (1 - 2 * mine) * (1 << bit)
        target = (other, where["ctx"]) if axis == "batch" else (where["batch"], other)
        return target, mine

    def bind(self, where, acc, recv, full, send_sem, recv_sem):
        self.acc, self.recv, self.full = acc, recv, full
        self.copies = []
        self.keeps = []
        for s, (base, size, order, slots) in enumerate(self.streams):
            off = base
            down, up, keeps = [], [], []
            for k, (axis, bit) in enumerate(order):
                target, mine = self.partner(where, axis, bit)
                half = size >> (k + 1)
                keep = pl.multiple_of(off + mine * half, TILE)
                away = pl.multiple_of(off + (1 - mine) * half, TILE)
                n = (s * self.levels + k) * 2
                down.append(pltpu.make_async_remote_copy(
                    src_ref=acc.at[pl.ds(away, half)], dst_ref=recv.at[pl.ds(slots[k], half)],
                    send_sem=send_sem.at[n], recv_sem=recv_sem.at[n],
                    device_id=target, device_id_type=MESH))
                up.append(pltpu.make_async_remote_copy(
                    src_ref=full.at[pl.ds(keep, half)], dst_ref=full.at[pl.ds(keep, half)],
                    send_sem=send_sem.at[n + 1], recv_sem=recv_sem.at[n + 1],
                    device_id=target, device_id_type=MESH))
                keeps.append((keep, half, slots[k]))
                off = keep
            self.copies.append((down, up))
            self.keeps.append(keeps)

    def begin(self):
        for down, _ in self.copies:
            down[0].start()

    def step(self, k):
        last = self.levels - 1
        for s, (down, up) in enumerate(self.copies):
            if k <= last:
                down[k].wait()
                keep, half, slot = self.keeps[s][k]
                total = self.acc[pl.ds(keep, half), :].astype(F32) + self.recv[pl.ds(slot, half), :].astype(F32)
                if k < last:
                    self.acc[pl.ds(keep, half), :] = total.astype(BF16)
                    down[k + 1].start()
                else:
                    self.full[pl.ds(keep, half), :] = total.astype(BF16)
                    up[last].start()
            else:
                n = 2 * self.levels - 1 - k
                up[n].wait()
                if n > 0:
                    up[n - 1].start()

    @property
    def steps(self):
        return 2 * self.levels


def position():
    return {"batch": lax.axis_index("batch"), "ctx": lax.axis_index("ctx")}


def middle(early, late, cap, batch_n, ctx_n,
           sums, amount, gout, pick, tags, er, u, x, b, dxl, tail, db, dc, w_up, w_in,
           gout_out, grads_out, arrived_out,
           e_acc, e_recv, e_full, e_send, e_got, l_acc, l_recv, l_full, l_send, l_got,
           other, other_amount, moving, entering, entering_other, carry, c_send, c_recv,
           rows, arrived, r_send, r_recv, own_sem):
    where = position()
    batch, ctx = where["batch"], where["ctx"]
    me = batch * ctx_n + ctx
    count = batch_n * ctx_n
    pair, place = ctx // 2, ctx % 2
    pairs = ctx_n // 2
    entering[...] = jnp.zeros_like(entering)
    partner = (batch, ctx + 1 - 2 * place)
    earlier = (batch, jnp.maximum(ctx - 2, 0))
    barrier = pltpu.get_barrier_semaphore()

    def at(step):
        to = (me + step) % count
        return to, (to // ctx_n, to % ctx_n)

    def hello(step, _):
        pl.semaphore_signal(barrier, inc=1, device_id=at(step)[1], device_id_type=MESH)
        return 0

    lax.fori_loop(1, count, hello, 0)
    e_acc[...] = gout[...]
    pl.semaphore_wait(barrier, count - 1)

    def send(src, dst, n, target):
        return pltpu.make_async_remote_copy(
            src_ref=src, dst_ref=dst, send_sem=c_send.at[n], recv_sem=c_recv.at[n],
            device_id=target, device_id_type=MESH)

    amounts = send(amount, other_amount, 0, partner)
    halves = send(sums.at[1 - place], other.at[1 - place], 1, partner)
    second = send(sums.at[1], other.at[1], 2, partner)
    hop = send(moving, entering, 3, earlier)
    cross = send(entering, entering_other, 4, partner)
    amounts.start()
    halves.start()

    early.bind(where, e_acc, e_recv, e_full, e_send, e_got)
    late.bind(where, l_acc, l_recv, l_full, l_send, l_got)
    early.begin()
    amounts.wait()
    halves.wait()

    @pl.when(place == 1)
    def _():
        second.start()

    mine = sums[place].astype(F32)
    theirs = other[place].astype(F32)
    a_mine = amount[place][0:1]
    a_theirs = other_amount[place][0:1]
    is_first = place == 0
    whole = jnp.where(is_first, mine + a_mine * theirs, theirs + a_theirs * mine)
    a_whole = a_mine * a_theirs
    done = 0
    for h in range(pairs - 2, -1, -1):
        @pl.when(pair == h + 1)
        def _():
            moving[...] = (whole + a_whole * entering[...].astype(F32)).astype(BF16)
            hop.start()

        if done < early.levels:
            early.step(done)
            done += 1

        @pl.when(pair == h)
        def _():
            hop.wait_recv()

    cross.start()
    early.step(done)
    done += 1
    cross.wait()

    @pl.when(place == 1)
    def _():
        second.wait_send()
        carry[1] = entering[...]
        carry[0] = entering_other[...]

    @pl.when(place == 0)
    def _():
        second.wait_recv()
        carry[0] = (other[0].astype(F32) + other_amount[0][0:1] * entering[...].astype(F32)).astype(BF16)
        carry[1] = (other[1].astype(F32) + other_amount[1][0:1] * entering_other[...].astype(F32)).astype(BF16)

    @pl.when(pair > 0)
    def _():
        hop.wait_send()

    du = back(er, u, x, b, dxl, tail, db, dc, carry, w_in, l_acc)
    late.begin()
    width = er.shape[1]
    rows[:, :width] = mm(pick[...], mm_t(du, w_up[...]).astype(BF16)).astype(BF16)
    rows[:, width:] = tags[...]
    own_rows = pl.ds(pl.multiple_of(me * cap, TILE), cap)
    own = pltpu.make_async_copy(rows.at[own_rows], arrived.at[own_rows], own_sem)
    own.start()

    def row_copy(step):
        to, target = at(step)
        return pltpu.make_async_remote_copy(
            src_ref=rows.at[pl.ds(pl.multiple_of(to * cap, TILE), cap)], dst_ref=arrived.at[own_rows],
            send_sem=r_send.at[step], recv_sem=r_recv.at[step],
            device_id=target, device_id_type=MESH)

    def launch(step, _):
        row_copy(step).start()
        return 0

    lax.fori_loop(1, count, launch, 0)
    for k in range(late.steps):
        late.step(k)
        if done < early.steps:
            early.step(done)
            done += 1
            if done == early.steps:
                gout_out[...] = e_full[...]

    def finish(step, _):
        row_copy(step).wait()
        return 0

    lax.fori_loop(1, count, finish, 0)
    own.wait()
    grads_out[...] = l_full[...]
    arrived_out[...] = arrived[...]


def local(event_rows, event_index, decay, saved_state, dout, w_up, w_in, w_out, skip):
    batch_n = lax.axis_size("batch")
    ctx_n = lax.axis_size("ctx")
    count = batch_n * ctx_n
    er = event_rows[0]
    tokens, width = er.shape
    inner, depth = w_out.shape
    proj = w_in.shape[1]
    state = (proj - inner) // 2
    heads = skip.shape[0]
    half = inner // 2
    cap = TILE
    shape = jax.ShapeDtypeStruct
    params = pltpu.CompilerParams(vmem_limit_bytes=LIMIT)
    gout_rows = inner * depth // LANES
    grad_rows = (width * depth + depth * proj) // LANES
    slots = count * cap
    held = jnp.swapaxes(saved_state[0, 0], 1, 2).reshape(inner, state)
    u, x, b, dxl, tail, db, dc, sums, amount, gout, pick, tags = pl.pallas_call(
        partial(front, cap),
        out_shape=(
            shape((tokens, depth), BF16), shape((tokens, inner), BF16), shape((tokens, state), BF16),
            shape((tokens, inner), F32), shape((tokens, inner), F32), shape((tokens, state), F32),
            shape((tokens, state), F32), shape((2, state, half), BF16), shape((2, 8, half), F32),
            shape((gout_rows, LANES), BF16), shape((slots, tokens), BF16), shape((slots, LANES), BF16),
        ),
        in_specs=[VMEM] * 8 + [SMEM],
        out_specs=[VMEM] * 12,
        scratch_shapes=[pltpu.VMEM((tokens, inner), BF16), pltpu.VMEM((heads, LANES), F32)],
        compiler_params=params,
        name="front",
    )(er, event_index, decay[0], held, dout[0], w_up, w_in, w_out, skip)

    early = Summing(gout_rows, batch_n, ctx_n)
    late = Summing(grad_rows, batch_n, ctx_n)
    gout, grads, arrived = pl.pallas_call(
        partial(middle, early, late, cap, batch_n, ctx_n),
        out_shape=(
            shape((gout_rows, LANES), BF16), shape((grad_rows, LANES), BF16),
            shape((slots, width + LANES), BF16),
        ),
        in_specs=[VMEM] * 15,
        out_specs=[VMEM] * 3,
        scratch_shapes=early.scratch(gout_rows) + late.scratch(grad_rows) + [
            pltpu.VMEM((2, state, half), BF16),
            pltpu.VMEM((2, 8, half), F32),
            pltpu.VMEM((state, half), BF16),
            pltpu.VMEM((state, half), BF16),
            pltpu.VMEM((state, half), BF16),
            pltpu.VMEM((2, state, half), BF16),
            pltpu.SemaphoreType.DMA((5,)),
            pltpu.SemaphoreType.DMA((5,)),
            pltpu.VMEM((slots, width + LANES), BF16),
            pltpu.VMEM((slots, width + LANES), BF16),
            pltpu.SemaphoreType.DMA((count,)),
            pltpu.SemaphoreType.DMA((count,)),
            pltpu.SemaphoreType.DMA,
        ],
        compiler_params=pltpu.CompilerParams(
            vmem_limit_bytes=LIMIT, collective_id=0, has_side_effects=True),
        name="middle",
    )(sums, amount, gout, pick, tags, er, u, x, b, dxl, tail, db, dc, w_up, w_in)

    grad_up, grad_in, grad_out, grad_skip, grad_table = pl.pallas_call(
        unpack,
        out_shape=(
            shape((width, depth), F32), shape((depth, proj), F32), shape((inner, depth), F32),
            shape((1, heads), F32), shape((ROWS_DEV, width), F32),
        ),
        in_specs=[VMEM] * 3,
        out_specs=[VMEM] * 5,
        compiler_params=params,
        name="unpack",
    )(gout, grads, arrived)
    return grad_up, grad_in, grad_out, grad_skip[0], grad_table


def solution(mesh):
    in_specs = (
        P("batch", "ctx", None),
        P("batch", "ctx"),
        P("batch", None, "ctx"),
        P("batch", "ctx", None, None, None),
        P("batch", "ctx", None),
        P(),
        P(),
        P(),
        P(),
    )
    out_specs = (P(), P(), P(), P(), P(("batch", "ctx"), None))
    return jax.shard_map(local, mesh=mesh, in_specs=in_specs, out_specs=out_specs, check_vma=False)
```

```python
from functools import partial

import jax
import jax.numpy as jnp
from jax import lax
from jax.experimental import pallas as pl
from jax.experimental.pallas import tpu as pltpu
from jax.sharding import PartitionSpec as P

ROWS_DEV = 512
ROWS_BITS = 9
STEP_SIZE = 0.0625
LANES = 128
TILE = 16
MESH = pl.DeviceIdType.MESH
F32 = jnp.float32
BF16 = jnp.bfloat16
VMEM = pl.BlockSpec(memory_space=pltpu.VMEM)
SMEM = pl.BlockSpec(memory_space=pltpu.SMEM)
LIMIT = 60 * 1024 * 1024


def mm(a, b):
    return lax.dot_general(a, b, (((1,), (0,)), ((), ())), preferred_element_type=F32)


def mm_t(a, b):
    return lax.dot_general(a, b, (((1,), (1,)), ((), ())), preferred_element_type=F32)


def t_mm(a, b):
    return lax.dot_general(a, b, (((0,), (0,)), ((), ())), preferred_element_type=F32)


def exact_mm_t(a, b):
    return lax.dot_general(
        a, b, (((1,), (1,)), ((), ())), precision=lax.Precision.HIGHEST, preferred_element_type=F32
    )


def cut(j):
    return slice(LANES * j, LANES * (j + 1))


def front(er, decay, dout, w_up, w_in, w_out, u_out, x_out, b_out, tail_out, sums_out, amount_out):
    tokens = er.shape[0]
    inner = w_out.shape[0]
    state = b_out.shape[1]
    heads = decay.shape[0]
    scale = state ** -0.5
    u = mm(er[...], w_up[...]).astype(BF16)
    u_out[...] = u
    proj = mm(u, w_in[...]).astype(BF16)
    x_out[...] = proj[:, :inner]
    b = proj[:, inner:inner + state]
    c = proj[:, inner + state:]
    b_out[...] = b
    dy = mm_t(dout[...], w_out[...]).astype(BF16)
    logs = jnp.log(decay[...])
    rows = lax.broadcasted_iota(jnp.int32, (tokens, tokens), 0)
    cols = lax.broadcasted_iota(jnp.int32, (tokens, tokens), 1)
    causal = rows >= cols
    tri = jnp.where(causal, 1.0, 0.0).astype(F32)
    cum_col = exact_mm_t(tri, logs)
    cum_row = exact_mm_t(logs, tri)
    total = cum_col[tokens - 1:tokens, :]
    start = jnp.exp(cum_col)
    tail = jnp.exp(total - cum_col)
    amount = jnp.exp(total)
    first = lax.broadcasted_iota(jnp.int32, (1, LANES), 1) < LANES // 2
    starts, sdys = [], []
    for j in range(heads // 2):
        def spread(a):
            return jnp.where(first, a[:, 2 * j:2 * j + 1], a[:, 2 * j + 1:2 * j + 2])

        starts.append(spread(start))
        tail_out[:, cut(j)] = spread(tail)
        sdy = (starts[j] * dy[:, cut(j)].astype(F32)).astype(BF16)
        sdys.append(sdy)
        half, k = j // (heads // 4), j % (heads // 4)
        sums_out[half, :, cut(k)] = (scale * t_mm(c, sdy)).astype(BF16)
        amount_out[half, :, cut(k)] = jnp.broadcast_to(spread(amount), (8, LANES))
    return proj, dy, cum_col, cum_row, causal, first, starts, sdys


def within(kept, hs, dout, skip, inner, dxl_out, db_out, dc_out, gout_out, y_buf, dsk):
    proj, dy, cum_col, cum_row, causal, first, starts, sdys = kept
    tokens = proj.shape[0]
    heads = cum_row.shape[0]
    state = db_out.shape[1]
    scale = state ** -0.5
    b = proj[:, inner:inner + state]
    c = proj[:, inner + state:]
    cb = jnp.where(causal, mm_t(c, b), 0.0)
    weight = jnp.zeros((tokens, tokens), F32)
    dc = jnp.zeros((tokens, state), F32)
    for j in range(heads // 2):
        xp = proj[:, cut(j)]
        dyp = dy[:, cut(j)]
        xf = xp.astype(F32)
        dyf = dyp.astype(F32)
        forward, backward = [], []
        prod = jnp.sum(xf * dyf, axis=0, keepdims=True)
        for i in range(2):
            h = 2 * j + i
            mine = first if i == 0 else jnp.logical_not(first)
            mask = jnp.exp(jnp.minimum(cum_col[:, h:h + 1] - cum_row[h:h + 1, :], 0.0))
            g = (mask * cb).astype(BF16)
            forward.append(mm(g, xp))
            backward.append(t_mm(g, dyp))
            weight += mask * mm_t(jnp.where(mine, dyf, 0.0).astype(BF16), xp)
            dsk[h:h + 1, :] = jnp.broadcast_to(
                jnp.sum(jnp.where(mine, prod, 0.0), axis=1, keepdims=True), (1, LANES))
        skip_p = jnp.where(first, skip[2 * j], skip[2 * j + 1])
        hs_p = hs[LANES * j:LANES * (j + 1), :].astype(BF16)
        inside = jnp.where(first, forward[0], forward[1])
        y = scale * (mm_t(c, hs_p) * starts[j] + STEP_SIZE * inside) + skip_p * xf
        y_buf[:, cut(j)] = y.astype(BF16)
        dxl_out[:, cut(j)] = (STEP_SIZE * scale) * jnp.where(first, backward[0], backward[1]) + skip_p * dyf
        dc += mm(sdys[j], hs_p)
    weight = jnp.where(causal, weight, 0.0).astype(BF16)
    dc_out[...] = scale * (dc + STEP_SIZE * mm(weight, b))
    db_out[...] = (STEP_SIZE * scale) * t_mm(weight, c)
    y_all = y_buf[...]
    for j in range(dout.shape[1] // LANES):
        gout_out[inner * j:inner * (j + 1), :] = t_mm(y_all, dout[:, cut(j)]).astype(BF16)


def route(cap, slots, idx_row, value):
    tokens = idx_row.shape[1]
    spread = jnp.broadcast_to(idx_row.astype(F32), (LANES, tokens))
    idx_col = spread.T[:, 0:1].astype(jnp.int32)
    owner_row = lax.shift_right_logical(idx_row, ROWS_BITS)
    owner_col = lax.shift_right_logical(idx_col, ROWS_BITS)
    earlier = lax.broadcasted_iota(jnp.int32, (tokens, tokens), 0) < lax.broadcasted_iota(
        jnp.int32, (tokens, tokens), 1)
    rank = jnp.sum(
        jnp.where(jnp.logical_and(earlier, owner_col == owner_row), 1.0, 0.0), axis=0, keepdims=True)
    slot = owner_row * cap + rank.astype(jnp.int32)
    pick = jnp.where(
        lax.broadcasted_iota(jnp.int32, (slots, tokens), 0) == slot, 1.0, 0.0).astype(BF16)
    number = idx_col - owner_col * ROWS_DEV + 1
    high = lax.shift_right_logical(number, 8)
    low = number - high * 256
    lane = lax.broadcasted_iota(jnp.int32, (tokens, LANES), 1)
    tags = jnp.where(lane == 0, high.astype(F32), jnp.where(lane == 1, low.astype(F32), 0.0))
    one = value.astype(BF16).astype(F32)
    two = (value - one).astype(BF16).astype(F32)
    three = value - one - two
    place = lax.broadcasted_iota(jnp.int32, value.shape, 1)
    share = jnp.where(place == 2, one, jnp.where(place == 3, two, jnp.where(place == 4, three, 0.0)))
    if cap > share.shape[0]:
        share = jnp.concatenate([share, jnp.zeros((cap - share.shape[0], LANES), F32)], axis=0)
    tagged = mm(pick, tags.astype(BF16)).reshape(slots // cap, cap, LANES) + share[None]
    return pick, tagged.reshape(slots, LANES).astype(BF16)


def back(er, u, x, b, dxl, tail, db, dc, carry, w_in, grads_out):
    carry_all = jnp.concatenate([carry[0], carry[1]], axis=1)
    tail_v = tail[...]
    dx = dxl[...] + STEP_SIZE * tail_v * mm(b[...], carry_all)
    dbv = db[...] + STEP_SIZE * mm_t((tail_v * x[...].astype(F32)).astype(BF16), carry_all)
    dproj = jnp.concatenate([dx.astype(BF16), dbv.astype(BF16), dc[...].astype(BF16)], axis=1)
    du = mm_t(dproj, w_in[...]).astype(BF16)
    erv = er[...]
    width = erv.shape[1]
    for j in range(du.shape[1] // LANES):
        grads_out[width * j:width * (j + 1), :] = t_mm(erv, du[:, cut(j)]).astype(BF16)
    base = width * (du.shape[1] // LANES)
    uv = u[...]
    depth = uv.shape[1]
    for j in range(dproj.shape[1] // LANES):
        grads_out[base + depth * j:base + depth * (j + 1), :] = t_mm(uv, dproj[:, cut(j)]).astype(BF16)
    return du


def unpack(gout, grads, arrived, grad_up, grad_in, grad_out, grad_skip, grad_table):
    inner = grad_out.shape[0]
    for j in range(grad_out.shape[1] // LANES):
        grad_out[:, cut(j)] = gout[inner * j:inner * (j + 1), :].astype(F32)
    width, depth = grad_up.shape
    for j in range(depth // LANES):
        grad_up[:, cut(j)] = grads[width * j:width * (j + 1), :].astype(F32)
    base = width * (depth // LANES)
    for j in range(grad_in.shape[1] // LANES):
        grad_in[:, cut(j)] = grads[base + depth * j:base + depth * (j + 1), :].astype(F32)
    tags = arrived[:, width:].astype(F32)
    number = tags[:, 0:1] * 256.0 + tags[:, 1:2] - 1.0
    slots = tags.shape[0]
    row = lax.broadcasted_iota(jnp.int32, (slots, ROWS_DEV), 1).astype(F32)
    pick = jnp.where(row == number, 1.0, 0.0).astype(BF16)
    grad_table[...] = t_mm(pick, arrived[:, :width])
    heads = grad_skip.shape[1]
    cap = TILE
    parts = jnp.sum(tags.reshape(slots // cap, cap, LANES), axis=0)[:heads]
    place = lax.broadcasted_iota(jnp.int32, parts.shape, 1)
    kept = jnp.where(jnp.logical_and(place >= 2, place <= 4), parts, 0.0)
    sums = jnp.sum(kept, axis=1, keepdims=True)
    same = lax.broadcasted_iota(jnp.int32, (heads, heads), 0) == lax.broadcasted_iota(
        jnp.int32, (heads, heads), 1)
    grad_skip[...] = jnp.sum(jnp.where(same, sums, 0.0), axis=0, keepdims=True)


def bit_count(n):
    return n.bit_length() - 1


class Summing:
    def __init__(self, rows, batch_n, ctx_n):
        self.names = [("batch", i) for i in range(bit_count(batch_n))]
        self.names += [("ctx", i) for i in range(bit_count(ctx_n))]
        self.levels = len(self.names)
        tiles = rows // (batch_n * ctx_n) // TILE
        self.streams = []
        base = 0
        recv = 0
        rest = self.names[1:]
        for s in range(3):
            mine = (tiles + 2 - s) // 3
            if mine == 0:
                continue
            turn = rest[:3]
            order = self.names[:1] + turn[s:] + turn[:s] + rest[3:]
            size = mine * TILE << self.levels
            slots = []
            for k in range(self.levels):
                slots.append(recv)
                recv += size >> (k + 1)
            self.streams.append((base, size, order, slots))
            base += size
        self.recv_rows = recv
        self.sems = len(self.streams) * self.levels * 2

    def scratch(self, rows):
        return [
            pltpu.VMEM((rows, LANES), BF16),
            pltpu.VMEM((self.recv_rows, LANES), BF16),
            pltpu.VMEM((rows, LANES), BF16),
            pltpu.SemaphoreType.DMA((self.sems,)),
            pltpu.SemaphoreType.DMA((self.sems,)),
        ]

    def partners(self, where):
        out = []
        for axis, bit in self.names:
            out.append(self.partner(where, axis, bit)[0])
        return out

    def partner(self, where, axis, bit):
        at = where[axis]
        mine = (at // (1 << bit)) % 2
        other = at + (1 - 2 * mine) * (1 << bit)
        target = (other, where["ctx"]) if axis == "batch" else (where["batch"], other)
        return target, mine

    def bind(self, where, acc, recv, full, send_sem, recv_sem):
        self.acc, self.recv, self.full = acc, recv, full
        self.copies = []
        self.keeps = []
        for s, (base, size, order, slots) in enumerate(self.streams):
            off = base
            down, up, keeps = [], [], []
            for k, (axis, bit) in enumerate(order):
                target, mine = self.partner(where, axis, bit)
                half = size >> (k + 1)
                keep = pl.multiple_of(off + mine * half, TILE)
                away = pl.multiple_of(off + (1 - mine) * half, TILE)
                n = (s * self.levels + k) * 2
                down.append(pltpu.make_async_remote_copy(
                    src_ref=acc.at[pl.ds(away, half)], dst_ref=recv.at[pl.ds(slots[k], half)],
                    send_sem=send_sem.at[n], recv_sem=recv_sem.at[n],
                    device_id=target, device_id_type=MESH))
                up.append(pltpu.make_async_remote_copy(
                    src_ref=full.at[pl.ds(keep, half)], dst_ref=full.at[pl.ds(keep, half)],
                    send_sem=send_sem.at[n + 1], recv_sem=recv_sem.at[n + 1],
                    device_id=target, device_id_type=MESH))
                keeps.append((keep, half, slots[k]))
                off = keep
            self.copies.append((down, up))
            self.keeps.append(keeps)

    def begin(self):
        for down, _ in self.copies:
            down[0].start()

    def step(self, k):
        last = self.levels - 1
        for s, (down, up) in enumerate(self.copies):
            if k <= last:
                down[k].wait()
                keep, half, slot = self.keeps[s][k]
                total = self.acc[pl.ds(keep, half), :].astype(F32) + self.recv[pl.ds(slot, half), :].astype(F32)
                if k < last:
                    self.acc[pl.ds(keep, half), :] = total.astype(BF16)
                    down[k + 1].start()
                else:
                    self.full[pl.ds(keep, half), :] = total.astype(BF16)
                    up[last].start()
            else:
                n = 2 * self.levels - 1 - k
                up[n].wait()
                if n > 0:
                    up[n - 1].start()

    @property
    def steps(self):
        return 2 * self.levels


def position():
    return {"batch": lax.axis_index("batch"), "ctx": lax.axis_index("ctx")}


def middle(early, late, cap, batch_n, ctx_n,
           er, idx, decay, hs, dout, w_up, w_in, w_out, skip,
           gout_out, grads_out, arrived_out,
           sums, amount, u, x, b, dxl, tail, db, dc, y_buf, dsk, pick_buf,
           e_acc, e_recv, e_full, e_send, e_got, l_acc, l_recv, l_full, l_send, l_got,
           other, other_amount, moving, entering, entering_other, carry, c_send, c_recv,
           rows, arrived, r_send, r_recv, own_sem):
    where = position()
    batch, ctx = where["batch"], where["ctx"]
    me = batch * ctx_n + ctx
    count = batch_n * ctx_n
    pair, place = ctx // 2, ctx % 2
    pairs = ctx_n // 2
    entering[...] = jnp.zeros_like(entering)
    partner = (batch, ctx + 1 - 2 * place)
    earlier = (batch, jnp.maximum(ctx - 2, 0))
    barrier = pltpu.get_barrier_semaphore()

    def at(step):
        to = (me + step) % count
        return to, (to // ctx_n, to % ctx_n)

    def hello(step, _):
        pl.semaphore_signal(barrier, inc=1, device_id=at(step)[1], device_id_type=MESH)
        return 0

    lax.fori_loop(1, count, hello, 0)
    kept = front(er, decay, dout, w_up, w_in, w_out, u, x, b, tail, sums, amount)
    pl.semaphore_wait(barrier, count - 1)

    def send(src, dst, n, target):
        return pltpu.make_async_remote_copy(
            src_ref=src, dst_ref=dst, send_sem=c_send.at[n], recv_sem=c_recv.at[n],
            device_id=target, device_id_type=MESH)

    amounts = send(amount, other_amount, 0, partner)
    halves = send(sums.at[1 - place], other.at[1 - place], 1, partner)
    second = send(sums.at[1], other.at[1], 2, partner)
    hop = send(moving, entering, 3, earlier)
    cross = send(entering, entering_other, 4, partner)
    amounts.start()
    halves.start()

    early.bind(where, e_acc, e_recv, e_full, e_send, e_got)
    late.bind(where, l_acc, l_recv, l_full, l_send, l_got)
    within(kept, hs, dout, skip, w_out.shape[0], dxl, db, dc, e_acc, y_buf, dsk)
    early.begin()
    width = er.shape[1]
    pick, tags = route(cap, rows.shape[0], idx[...], dsk[...])
    pick_buf[...] = pick
    rows[:, width:] = tags
    amounts.wait()
    halves.wait()

    @pl.when(place == 1)
    def _():
        second.start()

    mine = sums[place].astype(F32)
    theirs = other[place].astype(F32)
    a_mine = amount[place][0:1]
    a_theirs = other_amount[place][0:1]
    is_first = place == 0
    whole = jnp.where(is_first, mine + a_mine * theirs, theirs + a_theirs * mine)
    a_whole = a_mine * a_theirs
    done = 0
    for h in range(pairs - 2, -1, -1):
        @pl.when(pair == h + 1)
        def _():
            moving[...] = (whole + a_whole * entering[...].astype(F32)).astype(BF16)
            hop.start()

        if done < early.levels:
            early.step(done)
            done += 1

        @pl.when(pair == h)
        def _():
            hop.wait_recv()

    cross.start()
    early.step(done)
    done += 1
    cross.wait()

    @pl.when(place == 1)
    def _():
        second.wait_send()
        carry[1] = entering[...]
        carry[0] = entering_other[...]

    @pl.when(place == 0)
    def _():
        second.wait_recv()
        carry[0] = (other[0].astype(F32) + other_amount[0][0:1] * entering[...].astype(F32)).astype(BF16)
        carry[1] = (other[1].astype(F32) + other_amount[1][0:1] * entering_other[...].astype(F32)).astype(BF16)

    @pl.when(pair > 0)
    def _():
        hop.wait_send()

    du = back(er, u, x, b, dxl, tail, db, dc, carry, w_in, l_acc)
    late.begin()
    rows[:, :width] = mm(pick_buf[...], mm_t(du, w_up[...]).astype(BF16)).astype(BF16)
    own_rows = pl.ds(pl.multiple_of(me * cap, TILE), cap)
    own = pltpu.make_async_copy(rows.at[own_rows], arrived.at[own_rows], own_sem)
    own.start()

    def row_copy(step):
        to, target = at(step)
        return pltpu.make_async_remote_copy(
            src_ref=rows.at[pl.ds(pl.multiple_of(to * cap, TILE), cap)], dst_ref=arrived.at[own_rows],
            send_sem=r_send.at[step], recv_sem=r_recv.at[step],
            device_id=target, device_id_type=MESH)

    def launch(step, _):
        row_copy(step).start()
        return 0

    lax.fori_loop(1, count, launch, 0)
    for k in range(late.steps):
        late.step(k)
        if done < early.steps:
            early.step(done)
            done += 1
            if done == early.steps:
                gout_out[...] = e_full[...]

    def finish(step, _):
        row_copy(step).wait()
        return 0

    lax.fori_loop(1, count, finish, 0)
    own.wait()
    grads_out[...] = l_full[...]
    arrived_out[...] = arrived[...]


def local(event_rows, event_index, decay, saved_state, dout, w_up, w_in, w_out, skip):
    batch_n = lax.axis_size("batch")
    ctx_n = lax.axis_size("ctx")
    count = batch_n * ctx_n
    er = event_rows[0]
    tokens, width = er.shape
    inner, depth = w_out.shape
    proj = w_in.shape[1]
    state = (proj - inner) // 2
    heads = skip.shape[0]
    half = inner // 2
    cap = TILE
    shape = jax.ShapeDtypeStruct
    params = pltpu.CompilerParams(vmem_limit_bytes=LIMIT)
    gout_rows = inner * depth // LANES
    grad_rows = (width * depth + depth * proj) // LANES
    slots = count * cap
    held = jnp.swapaxes(saved_state[0, 0], 1, 2).reshape(inner, state)
    early = Summing(gout_rows, batch_n, ctx_n)
    late = Summing(grad_rows, batch_n, ctx_n)
    gout, grads, arrived = pl.pallas_call(
        partial(middle, early, late, cap, batch_n, ctx_n),
        out_shape=(
            shape((gout_rows, LANES), BF16), shape((grad_rows, LANES), BF16),
            shape((slots, width + LANES), BF16),
        ),
        in_specs=[VMEM] * 8 + [SMEM],
        out_specs=[VMEM] * 3,
        scratch_shapes=[
            pltpu.VMEM((2, state, half), BF16),
            pltpu.VMEM((2, 8, half), F32),
            pltpu.VMEM((tokens, depth), BF16),
            pltpu.VMEM((tokens, inner), BF16),
            pltpu.VMEM((tokens, state), BF16),
            pltpu.VMEM((tokens, inner), F32),
            pltpu.VMEM((tokens, inner), F32),
            pltpu.VMEM((tokens, state), F32),
            pltpu.VMEM((tokens, state), F32),
            pltpu.VMEM((tokens, inner), BF16),
            pltpu.VMEM((heads, LANES), F32),
            pltpu.VMEM((slots, tokens), BF16),
        ] + early.scratch(gout_rows) + late.scratch(grad_rows) + [
            pltpu.VMEM((2, state, half), BF16),
            pltpu.VMEM((2, 8, half), F32),
            pltpu.VMEM((state, half), BF16),
            pltpu.VMEM((state, half), BF16),
            pltpu.VMEM((state, half), BF16),
            pltpu.VMEM((2, state, half), BF16),
            pltpu.SemaphoreType.DMA((5,)),
            pltpu.SemaphoreType.DMA((5,)),
            pltpu.VMEM((slots, width + LANES), BF16),
            pltpu.VMEM((slots, width + LANES), BF16),
            pltpu.SemaphoreType.DMA((count,)),
            pltpu.SemaphoreType.DMA((count,)),
            pltpu.SemaphoreType.DMA,
        ],
        compiler_params=pltpu.CompilerParams(
            vmem_limit_bytes=LIMIT, collective_id=0, has_side_effects=True),
        name="middle",
    )(er, event_index, decay[0], held, dout[0], w_up, w_in, w_out, skip)

    grad_up, grad_in, grad_out, grad_skip, grad_table = pl.pallas_call(
        unpack,
        out_shape=(
            shape((width, depth), F32), shape((depth, proj), F32), shape((inner, depth), F32),
            shape((1, heads), F32), shape((ROWS_DEV, width), F32),
        ),
        in_specs=[VMEM] * 3,
        out_specs=[VMEM] * 5,
        compiler_params=params,
        name="unpack",
    )(gout, grads, arrived)
    return grad_up, grad_in, grad_out, grad_skip[0], grad_table


def solution(mesh):
    in_specs = (
        P("batch", "ctx", None),
        P("batch", "ctx"),
        P("batch", None, "ctx"),
        P("batch", "ctx", None, None, None),
        P("batch", "ctx", None),
        P(),
        P(),
        P(),
        P(),
    )
    out_specs = (P(), P(), P(), P(), P(("batch", "ctx"), None))
    return jax.shard_map(local, mesh=mesh, in_specs=in_specs, out_specs=out_specs, check_vma=False)
```

```python
from functools import partial

import jax
import jax.numpy as jnp
from jax import lax
from jax.experimental import pallas as pl
from jax.experimental.pallas import tpu as pltpu
from jax.sharding import PartitionSpec as P

ROWS_DEV = 512
ROWS_BITS = 9
STEP_SIZE = 0.0625
LANES = 128
TILE = 16
MESH = pl.DeviceIdType.MESH
F32 = jnp.float32
BF16 = jnp.bfloat16
VMEM = pl.BlockSpec(memory_space=pltpu.VMEM)
SMEM = pl.BlockSpec(memory_space=pltpu.SMEM)
LIMIT = 60 * 1024 * 1024


def mm(a, b):
    return lax.dot_general(a, b, (((1,), (0,)), ((), ())), preferred_element_type=F32)


def mm_t(a, b):
    return lax.dot_general(a, b, (((1,), (1,)), ((), ())), preferred_element_type=F32)


def t_mm(a, b):
    return lax.dot_general(a, b, (((0,), (0,)), ((), ())), preferred_element_type=F32)


def exact_mm_t(a, b):
    return lax.dot_general(
        a, b, (((1,), (1,)), ((), ())), precision=lax.Precision.HIGHEST, preferred_element_type=F32
    )


def cut(j):
    return slice(LANES * j, LANES * (j + 1))


def front(er, decay, dout, w_up, w_in, w_out, u_out, x_out, b_out, tail_out, sums_out, amount_out):
    tokens = er.shape[0]
    inner = w_out.shape[0]
    state = b_out.shape[1]
    heads = decay.shape[0]
    scale = state ** -0.5
    u = mm(er[...], w_up[...]).astype(BF16)
    u_out[...] = u
    proj = mm(u, w_in[...]).astype(BF16)
    x_out[...] = proj[:, :inner]
    b = proj[:, inner:inner + state]
    c = proj[:, inner + state:]
    b_out[...] = b
    dy = mm_t(dout[...], w_out[...]).astype(BF16)
    logs = jnp.log(decay[...])
    rows = lax.broadcasted_iota(jnp.int32, (tokens, tokens), 0)
    cols = lax.broadcasted_iota(jnp.int32, (tokens, tokens), 1)
    causal = rows >= cols
    tri = jnp.where(causal, 1.0, 0.0).astype(F32)
    cum_col = exact_mm_t(tri, logs)
    cum_row = exact_mm_t(logs, tri)
    total = cum_col[tokens - 1:tokens, :]
    start = jnp.exp(cum_col)
    tail = jnp.exp(total - cum_col)
    amount = jnp.exp(total)
    first = lax.broadcasted_iota(jnp.int32, (1, LANES), 1) < LANES // 2
    starts, sdys = [], []
    for j in range(heads // 2):
        def spread(a):
            return jnp.where(first, a[:, 2 * j:2 * j + 1], a[:, 2 * j + 1:2 * j + 2])

        starts.append(spread(start))
        tail_out[:, cut(j)] = spread(tail)
        sdy = (starts[j] * dy[:, cut(j)].astype(F32)).astype(BF16)
        sdys.append(sdy)
        half, k = j // (heads // 4), j % (heads // 4)
        sums_out[half, :, cut(k)] = (scale * t_mm(c, sdy)).astype(BF16)
        amount_out[half, :, cut(k)] = jnp.broadcast_to(spread(amount), (8, LANES))
    return proj, dy, cum_col, cum_row, causal, first, starts, sdys


def within(kept, hs, dout, skip, inner, dxl_out, db_out, dc_out, gout_out, y_buf, dsk):
    proj, dy, cum_col, cum_row, causal, first, starts, sdys = kept
    tokens = proj.shape[0]
    heads = cum_row.shape[0]
    state = db_out.shape[1]
    scale = state ** -0.5
    b = proj[:, inner:inner + state]
    c = proj[:, inner + state:]
    cb = jnp.where(causal, mm_t(c, b), 0.0)
    weight = jnp.zeros((tokens, tokens), F32)
    dc = jnp.zeros((tokens, state), F32)
    for j in range(heads // 2):
        xp = proj[:, cut(j)]
        dyp = dy[:, cut(j)]
        xf = xp.astype(F32)
        dyf = dyp.astype(F32)
        forward, backward = [], []
        prod = jnp.sum(xf * dyf, axis=0, keepdims=True)
        for i in range(2):
            h = 2 * j + i
            mine = first if i == 0 else jnp.logical_not(first)
            mask = jnp.exp(jnp.minimum(cum_col[:, h:h + 1] - cum_row[h:h + 1, :], 0.0))
            g = (mask * cb).astype(BF16)
            forward.append(mm(g, xp))
            backward.append(t_mm(g, dyp))
            weight += mask * mm_t(jnp.where(mine, dyf, 0.0).astype(BF16), xp)
            dsk[h:h + 1, :] = jnp.broadcast_to(
                jnp.sum(jnp.where(mine, prod, 0.0), axis=1, keepdims=True), (1, LANES))
        skip_p = jnp.where(first, skip[2 * j], skip[2 * j + 1])
        hs_p = hs[LANES * j:LANES * (j + 1), :].astype(BF16)
        inside = jnp.where(first, forward[0], forward[1])
        y = scale * (mm_t(c, hs_p) * starts[j] + STEP_SIZE * inside) + skip_p * xf
        y_buf[:, cut(j)] = y.astype(BF16)
        dxl_out[:, cut(j)] = (STEP_SIZE * scale) * jnp.where(first, backward[0], backward[1]) + skip_p * dyf
        dc += mm(sdys[j], hs_p)
    weight = jnp.where(causal, weight, 0.0).astype(BF16)
    dc_out[...] = scale * (dc + STEP_SIZE * mm(weight, b))
    db_out[...] = (STEP_SIZE * scale) * t_mm(weight, c)
    y_all = y_buf[...]
    for j in range(dout.shape[1] // LANES):
        gout_out[inner * j:inner * (j + 1), :] = t_mm(y_all, dout[:, cut(j)]).astype(BF16)


def route(cap, slots, idx_row, value):
    tokens = idx_row.shape[1]
    spread = jnp.broadcast_to(idx_row.astype(F32), (LANES, tokens))
    idx_col = spread.T[:, 0:1].astype(jnp.int32)
    owner_row = lax.shift_right_logical(idx_row, ROWS_BITS)
    owner_col = lax.shift_right_logical(idx_col, ROWS_BITS)
    earlier = lax.broadcasted_iota(jnp.int32, (tokens, tokens), 0) < lax.broadcasted_iota(
        jnp.int32, (tokens, tokens), 1)
    rank = jnp.sum(
        jnp.where(jnp.logical_and(earlier, owner_col == owner_row), 1.0, 0.0), axis=0, keepdims=True)
    slot = owner_row * cap + rank.astype(jnp.int32)
    pick = jnp.where(
        lax.broadcasted_iota(jnp.int32, (slots, tokens), 0) == slot, 1.0, 0.0).astype(BF16)
    number = idx_col - owner_col * ROWS_DEV + 1
    high = lax.shift_right_logical(number, 8)
    low = number - high * 256
    lane = lax.broadcasted_iota(jnp.int32, (tokens, LANES), 1)
    tags = jnp.where(lane == 0, high.astype(F32), jnp.where(lane == 1, low.astype(F32), 0.0))
    one = value.astype(BF16).astype(F32)
    two = (value - one).astype(BF16).astype(F32)
    three = value - one - two
    place = lax.broadcasted_iota(jnp.int32, value.shape, 1)
    share = jnp.where(place == 2, one, jnp.where(place == 3, two, jnp.where(place == 4, three, 0.0)))
    if cap > share.shape[0]:
        share = jnp.concatenate([share, jnp.zeros((cap - share.shape[0], LANES), F32)], axis=0)
    tagged = mm(pick, tags.astype(BF16)).reshape(slots // cap, cap, LANES) + share[None]
    return pick, tagged.reshape(slots, LANES).astype(BF16)


def back(beside, er, u, x, b, dxl, tail, db, dc, carry, w_in, grads_out):
    carry_all = jnp.concatenate([carry[0], carry[1]], axis=1)
    tail_v = tail[...]
    dx = dxl[...] + STEP_SIZE * tail_v * mm(b[...], carry_all)
    dbv = db[...] + STEP_SIZE * mm_t((tail_v * x[...].astype(F32)).astype(BF16), carry_all)
    dproj = jnp.concatenate([dx.astype(BF16), dbv.astype(BF16), dc[...].astype(BF16)], axis=1)
    beside()
    du = mm_t(dproj, w_in[...]).astype(BF16)
    erv = er[...]
    width = erv.shape[1]
    for j in range(du.shape[1] // LANES):
        grads_out[width * j:width * (j + 1), :] = t_mm(erv, du[:, cut(j)]).astype(BF16)
    base = width * (du.shape[1] // LANES)
    uv = u[...]
    depth = uv.shape[1]
    for j in range(dproj.shape[1] // LANES):
        grads_out[base + depth * j:base + depth * (j + 1), :] = t_mm(uv, dproj[:, cut(j)]).astype(BF16)
    return du


def unpack(gout, grads, arrived, grad_up, grad_in, grad_out, grad_skip, grad_table):
    inner = grad_out.shape[0]
    for j in range(grad_out.shape[1] // LANES):
        grad_out[:, cut(j)] = gout[inner * j:inner * (j + 1), :].astype(F32)
    width, depth = grad_up.shape
    for j in range(depth // LANES):
        grad_up[:, cut(j)] = grads[width * j:width * (j + 1), :].astype(F32)
    base = width * (depth // LANES)
    for j in range(grad_in.shape[1] // LANES):
        grad_in[:, cut(j)] = grads[base + depth * j:base + depth * (j + 1), :].astype(F32)
    tags = arrived[:, width:].astype(F32)
    number = tags[:, 0:1] * 256.0 + tags[:, 1:2] - 1.0
    slots = tags.shape[0]
    row = lax.broadcasted_iota(jnp.int32, (slots, ROWS_DEV), 1).astype(F32)
    pick = jnp.where(row == number, 1.0, 0.0).astype(BF16)
    grad_table[...] = t_mm(pick, arrived[:, :width])
    heads = grad_skip.shape[1]
    cap = TILE
    parts = jnp.sum(tags.reshape(slots // cap, cap, LANES), axis=0)[:heads]
    place = lax.broadcasted_iota(jnp.int32, parts.shape, 1)
    kept = jnp.where(jnp.logical_and(place >= 2, place <= 4), parts, 0.0)
    sums = jnp.sum(kept, axis=1, keepdims=True)
    same = lax.broadcasted_iota(jnp.int32, (heads, heads), 0) == lax.broadcasted_iota(
        jnp.int32, (heads, heads), 1)
    grad_skip[...] = jnp.sum(jnp.where(same, sums, 0.0), axis=0, keepdims=True)


def bit_count(n):
    return n.bit_length() - 1


class Summing:
    def __init__(self, rows, batch_n, ctx_n):
        names = [("batch", i) for i in range(bit_count(batch_n))]
        names += [("ctx", i) for i in range(bit_count(ctx_n))]
        rest = names[1:]
        self.levels = len(names) - 1
        tiles = rows // (batch_n * ctx_n) // TILE
        self.streams = []
        base = 0
        recv = 0
        self.sems = 0
        for s in range(3):
            mine = (tiles + 2 - s) // 3
            if mine == 0:
                continue
            turn = rest[:3]
            turn = turn[s:] + turn[:s]
            groups = [names[:1], turn[:1], turn[1:2], turn[2:3] + rest[3:4]]
            groups += [[name] for name in rest[4:]]
            size = mine * TILE << len(names)
            plan = []
            part = size
            for group in groups:
                part //= 1 << len(group)
                others = (1 << len(group)) - 1
                plan.append((group, part, recv, self.sems))
                recv += part * others
                self.sems += 2 * others
            self.streams.append((base, plan))
            base += size
        self.recv_rows = recv

    def scratch(self, rows):
        return [
            pltpu.VMEM((rows, LANES), BF16),
            pltpu.VMEM((self.recv_rows, LANES), BF16),
            pltpu.VMEM((rows, LANES), BF16),
            pltpu.SemaphoreType.DMA((self.sems,)),
            pltpu.SemaphoreType.DMA((self.sems,)),
        ]

    def bind(self, where, acc, recv, full, send_sem, recv_sem):
        self.acc, self.recv, self.full = acc, recv, full
        self.copies = []
        self.keeps = []
        for base, plan in self.streams:
            off = base
            down, up, keeps = [], [], []
            for group, part, slot, sem in plan:
                members = 1 << len(group)
                bits = [(where[axis] // (1 << bit)) % 2 for axis, bit in group]
                mine = sum(value * (1 << n) for n, value in enumerate(bits))
                keep = pl.multiple_of(off + mine * part, TILE)
                downs, ups = [], []
                for d in range(1, members):
                    member = (mine + d) % members
                    at = dict(where)
                    for n, (axis, bit) in enumerate(group):
                        at[axis] = at[axis] + ((member // (1 << n)) % 2 - bits[n]) * (1 << bit)
                    target = (at["batch"], at["ctx"])
                    away = pl.multiple_of(off + member * part, TILE)
                    n = sem + 2 * (d - 1)
                    downs.append(pltpu.make_async_remote_copy(
                        src_ref=acc.at[pl.ds(away, part)],
                        dst_ref=recv.at[pl.ds(slot + (d - 1) * part, part)],
                        send_sem=send_sem.at[n], recv_sem=recv_sem.at[n],
                        device_id=target, device_id_type=MESH))
                    ups.append(pltpu.make_async_remote_copy(
                        src_ref=full.at[pl.ds(keep, part)], dst_ref=full.at[pl.ds(keep, part)],
                        send_sem=send_sem.at[n + 1], recv_sem=recv_sem.at[n + 1],
                        device_id=target, device_id_type=MESH))
                down.append(downs)
                up.append(ups)
                keeps.append((keep, part, slot))
                off = keep
            self.copies.append((down, up))
            self.keeps.append(keeps)

    def begin(self):
        for down, _ in self.copies:
            for copy in down[0]:
                copy.start()

    def step(self, k):
        last = self.levels - 1
        for s, (down, up) in enumerate(self.copies):
            if k <= last:
                keep, part, slot = self.keeps[s][k]
                total = self.acc[pl.ds(keep, part), :].astype(F32)
                for n, copy in enumerate(down[k]):
                    copy.wait()
                    total += self.recv[pl.ds(slot + n * part, part), :].astype(F32)
                if k < last:
                    self.acc[pl.ds(keep, part), :] = total.astype(BF16)
                else:
                    self.full[pl.ds(keep, part), :] = total.astype(BF16)
                following = down[k + 1] if k < last else up[last]
            else:
                n = 2 * self.levels - 1 - k
                for copy in up[n]:
                    copy.wait()
                following = up[n - 1] if n > 0 else []
            for copy in following:
                copy.start()

    @property
    def steps(self):
        return 2 * self.levels


def joined(ref):
    return jnp.concatenate([ref[n] for n in range(ref.shape[0])], axis=1)


def position():
    return {"batch": lax.axis_index("batch"), "ctx": lax.axis_index("ctx")}


def middle(early, late, cap, batch_n, ctx_n,
           er, idx, decay, hs, dout, w_up, w_in, w_out, skip,
           gout_out, grads_out, arrived_out,
           sums, amount, u, x, b, dxl, tail, db, dc, y_buf, dsk, pick_buf,
           e_acc, e_recv, e_full, e_send, e_got, l_acc, l_recv, l_full, l_send, l_got,
           other, other_amount, moving, entering, entering_other, carry, c_send, c_recv,
           rows, arrived, r_send, r_recv, own_sem, out_sems):
    where = position()
    batch, ctx = where["batch"], where["ctx"]
    me = batch * ctx_n + ctx
    count = batch_n * ctx_n
    pair, place = ctx // 2, ctx % 2
    pairs = ctx_n // 2
    entering[...] = jnp.zeros_like(entering)
    partner = (batch, ctx + 1 - 2 * place)
    earlier = (batch, jnp.maximum(ctx - 2, 0))
    barrier = pltpu.get_barrier_semaphore()

    def at(step):
        to = (me + step) % count
        return to, (to // ctx_n, to % ctx_n)

    def hello(step, _):
        pl.semaphore_signal(barrier, inc=1, device_id=at(step)[1], device_id_type=MESH)
        return 0

    lax.fori_loop(1, count, hello, 0)
    kept = front(er, decay, dout, w_up, w_in, w_out, u, x, b, tail, sums, amount)
    pl.semaphore_wait(barrier, count - 1)

    def send(src, dst, n, target):
        return pltpu.make_async_remote_copy(
            src_ref=src, dst_ref=dst, send_sem=c_send.at[n], recv_sem=c_recv.at[n],
            device_id=target, device_id_type=MESH)

    amounts = send(amount, other_amount, 0, partner)
    halves = send(sums.at[1 - place], other.at[1 - place], 1, partner)
    second = send(sums.at[1], other.at[1], 2, partner)
    hops = [send(moving.at[n], entering.at[n], 5 + n, earlier) for n in range(entering.shape[0])]
    span = entering.shape[2]
    cross = send(entering, entering_other, 4, partner)
    amounts.start()
    halves.start()

    early.bind(where, e_acc, e_recv, e_full, e_send, e_got)
    late.bind(where, l_acc, l_recv, l_full, l_send, l_got)
    within(kept, hs, dout, skip, w_out.shape[0], dxl, db, dc, e_acc, y_buf, dsk)
    early.begin()
    width = er.shape[1]
    pick, tags = route(cap, rows.shape[0], idx[...], dsk[...])
    pick_buf[...] = pick
    rows[:, width:] = tags
    amounts.wait()
    halves.wait()

    @pl.when(place == 1)
    def _():
        second.start()

    mine = sums[place].astype(F32)
    theirs = other[place].astype(F32)
    a_mine = amount[place][0:1]
    a_theirs = other_amount[place][0:1]
    is_first = place == 0
    whole = jnp.where(is_first, mine + a_mine * theirs, theirs + a_theirs * mine)
    a_whole = a_mine * a_theirs
    done = 0
    for h in range(pairs - 2, -1, -1):
        @pl.when(pair == h + 1)
        def _():
            for n, hop in enumerate(hops):
                if h + 1 < pairs - 1:
                    hop.wait_recv()
                piece = slice(n * span, (n + 1) * span)
                moving[n] = (whole[:, piece] + a_whole[:, piece] * entering[n].astype(F32)).astype(BF16)
                hop.start()

        if done < early.levels:
            early.step(done)
            done += 1

    @pl.when(pair == 0)
    def _():
        for hop in hops:
            hop.wait_recv()

    cross.start()
    early.step(done)
    done += 1
    cross.wait()

    @pl.when(place == 1)
    def _():
        second.wait_send()
        carry[1] = joined(entering)
        carry[0] = joined(entering_other)

    @pl.when(place == 0)
    def _():
        second.wait_recv()
        carry[0] = (other[0].astype(F32) + other_amount[0][0:1] * joined(entering).astype(F32)).astype(BF16)
        carry[1] = (other[1].astype(F32) + other_amount[1][0:1] * joined(entering_other).astype(F32)).astype(BF16)

    @pl.when(pair > 0)
    def _():
        for hop in hops:
            hop.wait_send()

    du = back(lambda: early.step(done), er, u, x, b, dxl, tail, db, dc, carry, w_in, l_acc)
    done += 1
    late.begin()
    rows[:, :width] = mm(pick_buf[...], mm_t(du, w_up[...]).astype(BF16)).astype(BF16)
    own_rows = pl.ds(pl.multiple_of(me * cap, TILE), cap)
    own = pltpu.make_async_copy(rows.at[own_rows], arrived.at[own_rows], own_sem)
    own.start()

    def row_copy(step):
        to, target = at(step)
        return pltpu.make_async_remote_copy(
            src_ref=rows.at[pl.ds(pl.multiple_of(to * cap, TILE), cap)], dst_ref=arrived.at[own_rows],
            send_sem=r_send.at[step], recv_sem=r_recv.at[step],
            device_id=target, device_id_type=MESH)

    def launch(step, _):
        row_copy(step).start()
        return 0

    lax.fori_loop(1, count, launch, 0)
    gout_copy = pltpu.make_async_copy(e_full, gout_out, out_sems.at[0])
    grads_copy = pltpu.make_async_copy(l_full, grads_out, out_sems.at[1])
    rows_done = pltpu.make_async_copy(arrived, arrived_out, out_sems.at[2])
    for k in range(late.steps):
        late.step(k)
        if done < early.steps:
            early.step(done)
            done += 1
            if done == early.steps:
                gout_copy.start()

    def finish(step, _):
        row_copy(step).wait()
        return 0

    grads_copy.start()
    lax.fori_loop(1, count, finish, 0)
    own.wait()
    rows_done.start()
    gout_copy.wait()
    grads_copy.wait()
    rows_done.wait()


def local(event_rows, event_index, decay, saved_state, dout, w_up, w_in, w_out, skip):
    batch_n = lax.axis_size("batch")
    ctx_n = lax.axis_size("ctx")
    count = batch_n * ctx_n
    er = event_rows[0]
    tokens, width = er.shape
    inner, depth = w_out.shape
    proj = w_in.shape[1]
    state = (proj - inner) // 2
    heads = skip.shape[0]
    half = inner // 2
    cap = TILE
    shape = jax.ShapeDtypeStruct
    params = pltpu.CompilerParams(vmem_limit_bytes=LIMIT)
    gout_rows = inner * depth // LANES
    grad_rows = (width * depth + depth * proj) // LANES
    slots = count * cap
    held = jnp.swapaxes(saved_state[0, 0], 1, 2).reshape(inner, state)
    early = Summing(gout_rows, batch_n, ctx_n)
    late = Summing(grad_rows, batch_n, ctx_n)
    gout, grads, arrived = pl.pallas_call(
        partial(middle, early, late, cap, batch_n, ctx_n),
        out_shape=(
            shape((gout_rows, LANES), BF16), shape((grad_rows, LANES), BF16),
            shape((slots, width + LANES), BF16),
        ),
        in_specs=[VMEM] * 8 + [SMEM],
        out_specs=[pl.BlockSpec(memory_space=pl.ANY)] * 3,
        scratch_shapes=[
            pltpu.VMEM((2, state, half), BF16),
            pltpu.VMEM((2, 8, half), F32),
            pltpu.VMEM((tokens, depth), BF16),
            pltpu.VMEM((tokens, inner), BF16),
            pltpu.VMEM((tokens, state), BF16),
            pltpu.VMEM((tokens, inner), F32),
            pltpu.VMEM((tokens, inner), F32),
            pltpu.VMEM((tokens, state), F32),
            pltpu.VMEM((tokens, state), F32),
            pltpu.VMEM((tokens, inner), BF16),
            pltpu.VMEM((heads, LANES), F32),
            pltpu.VMEM((slots, tokens), BF16),
        ] + early.scratch(gout_rows) + late.scratch(grad_rows) + [
            pltpu.VMEM((2, state, half), BF16),
            pltpu.VMEM((2, 8, half), F32),
            pltpu.VMEM((2, state, half // 2), BF16),
            pltpu.VMEM((2, state, half // 2), BF16),
            pltpu.VMEM((2, state, half // 2), BF16),
            pltpu.VMEM((2, state, half), BF16),
            pltpu.SemaphoreType.DMA((7,)),
            pltpu.SemaphoreType.DMA((7,)),
            pltpu.VMEM((slots, width + LANES), BF16),
            pltpu.VMEM((slots, width + LANES), BF16),
            pltpu.SemaphoreType.DMA((count,)),
            pltpu.SemaphoreType.DMA((count,)),
            pltpu.SemaphoreType.DMA,
            pltpu.SemaphoreType.DMA((3,)),
        ],
        compiler_params=pltpu.CompilerParams(
            vmem_limit_bytes=LIMIT, collective_id=0, has_side_effects=True),
        name="middle",
    )(er, event_index, decay[0], held, dout[0], w_up, w_in, w_out, skip)

    grad_up, grad_in, grad_out, grad_skip, grad_table = pl.pallas_call(
        unpack,
        out_shape=(
            shape((width, depth), F32), shape((depth, proj), F32), shape((inner, depth), F32),
            shape((1, heads), F32), shape((ROWS_DEV, width), F32),
        ),
        in_specs=[VMEM] * 3,
        out_specs=[VMEM] * 5,
        compiler_params=params,
        name="unpack",
    )(gout, grads, arrived)
    return grad_up, grad_in, grad_out, grad_skip[0], grad_table


def solution(mesh):
    in_specs = (
        P("batch", "ctx", None),
        P("batch", "ctx"),
        P("batch", None, "ctx"),
        P("batch", "ctx", None, None, None),
        P("batch", "ctx", None),
        P(),
        P(),
        P(),
        P(),
    )
    out_specs = (P(), P(), P(), P(), P(("batch", "ctx"), None))
    return jax.shard_map(local, mesh=mesh, in_specs=in_specs, out_specs=out_specs, check_vma=False)
```

```python
from functools import partial

import jax
import jax.numpy as jnp
from jax import lax
from jax.experimental import pallas as pl
from jax.experimental.pallas import tpu as pltpu
from jax.sharding import PartitionSpec as P

ROWS_DEV = 512
ROWS_BITS = 9
STEP_SIZE = 0.0625
LANES = 128
TILE = 16
MESH = pl.DeviceIdType.MESH
F32 = jnp.float32
BF16 = jnp.bfloat16
VMEM = pl.BlockSpec(memory_space=pltpu.VMEM)
SMEM = pl.BlockSpec(memory_space=pltpu.SMEM)
LIMIT = 60 * 1024 * 1024


def mm(a, b):
    return lax.dot_general(a, b, (((1,), (0,)), ((), ())), preferred_element_type=F32)


def mm_t(a, b):
    return lax.dot_general(a, b, (((1,), (1,)), ((), ())), preferred_element_type=F32)


def t_mm(a, b):
    return lax.dot_general(a, b, (((0,), (0,)), ((), ())), preferred_element_type=F32)


def exact_mm_t(a, b):
    return lax.dot_general(
        a, b, (((1,), (1,)), ((), ())), precision=lax.Precision.HIGHEST, preferred_element_type=F32
    )


def cut(j):
    return slice(LANES * j, LANES * (j + 1))


def front(er, decay, dout, w_up, w_in, w_out, u_out, x_out, b_out, tail_out, sums_out, amount_out):
    tokens = er.shape[0]
    inner = w_out.shape[0]
    state = b_out.shape[1]
    heads = decay.shape[0]
    scale = state ** -0.5
    u = mm(er[...], w_up[...]).astype(BF16)
    u_out[...] = u
    proj = mm(u, w_in[...]).astype(BF16)
    x_out[...] = proj[:, :inner]
    b = proj[:, inner:inner + state]
    c = proj[:, inner + state:]
    b_out[...] = b
    dy = mm_t(dout[...], w_out[...]).astype(BF16)
    logs = jnp.log(decay[...])
    rows = lax.broadcasted_iota(jnp.int32, (tokens, tokens), 0)
    cols = lax.broadcasted_iota(jnp.int32, (tokens, tokens), 1)
    causal = rows >= cols
    tri = jnp.where(causal, 1.0, 0.0).astype(F32)
    cum_col = exact_mm_t(tri, logs)
    cum_row = exact_mm_t(logs, tri)
    total = cum_col[tokens - 1:tokens, :]
    start = jnp.exp(cum_col)
    tail = jnp.exp(total - cum_col)
    amount = jnp.exp(total)
    first = lax.broadcasted_iota(jnp.int32, (1, LANES), 1) < LANES // 2
    starts, sdys = [], []
    for j in range(heads // 2):
        def spread(a):
            return jnp.where(first, a[:, 2 * j:2 * j + 1], a[:, 2 * j + 1:2 * j + 2])

        starts.append(spread(start))
        tail_out[:, cut(j)] = spread(tail)
        sdy = (starts[j] * dy[:, cut(j)].astype(F32)).astype(BF16)
        sdys.append(sdy)
        half, k = j // (heads // 4), j % (heads // 4)
        sums_out[half, :, cut(k)] = (scale * t_mm(c, sdy)).astype(BF16)
        amount_out[half, :, cut(k)] = jnp.broadcast_to(spread(amount), (8, LANES))
    return proj, dy, cum_col, cum_row, causal, first, starts, sdys


def within(kept, hs, dout, skip, inner, dxl_out, db_out, dc_out, gout_out, y_buf, dsk):
    proj, dy, cum_col, cum_row, causal, first, starts, sdys = kept
    tokens = proj.shape[0]
    heads = cum_row.shape[0]
    state = db_out.shape[1]
    scale = state ** -0.5
    b = proj[:, inner:inner + state]
    c = proj[:, inner + state:]
    cb = jnp.where(causal, mm_t(c, b), 0.0)
    weight = jnp.zeros((tokens, tokens), F32)
    dc = jnp.zeros((tokens, state), F32)
    for j in range(heads // 2):
        xp = proj[:, cut(j)]
        dyp = dy[:, cut(j)]
        xf = xp.astype(F32)
        dyf = dyp.astype(F32)
        forward, backward = [], []
        prod = jnp.sum(xf * dyf, axis=0, keepdims=True)
        for i in range(2):
            h = 2 * j + i
            mine = first if i == 0 else jnp.logical_not(first)
            mask = jnp.exp(jnp.minimum(cum_col[:, h:h + 1] - cum_row[h:h + 1, :], 0.0))
            g = (mask * cb).astype(BF16)
            forward.append(mm(g, xp))
            backward.append(t_mm(g, dyp))
            weight += mask * mm_t(jnp.where(mine, dyf, 0.0).astype(BF16), xp)
            dsk[h:h + 1, :] = jnp.broadcast_to(
                jnp.sum(jnp.where(mine, prod, 0.0), axis=1, keepdims=True), (1, LANES))
        skip_p = jnp.where(first, skip[2 * j], skip[2 * j + 1])
        hs_p = hs[LANES * j:LANES * (j + 1), :].astype(BF16)
        inside = jnp.where(first, forward[0], forward[1])
        y = scale * (mm_t(c, hs_p) * starts[j] + STEP_SIZE * inside) + skip_p * xf
        y_buf[:, cut(j)] = y.astype(BF16)
        dxl_out[:, cut(j)] = (STEP_SIZE * scale) * jnp.where(first, backward[0], backward[1]) + skip_p * dyf
        dc += mm(sdys[j], hs_p)
    weight = jnp.where(causal, weight, 0.0).astype(BF16)
    dc_out[...] = scale * (dc + STEP_SIZE * mm(weight, b))
    db_out[...] = (STEP_SIZE * scale) * t_mm(weight, c)
    y_all = y_buf[...]
    for j in range(dout.shape[1] // LANES):
        gout_out[inner * j:inner * (j + 1), :] = t_mm(y_all, dout[:, cut(j)]).astype(BF16)


def route(cap, slots, idx_row, value):
    tokens = idx_row.shape[1]
    spread = jnp.broadcast_to(idx_row.astype(F32), (LANES, tokens))
    idx_col = spread.T[:, 0:1].astype(jnp.int32)
    owner_row = lax.shift_right_logical(idx_row, ROWS_BITS)
    owner_col = lax.shift_right_logical(idx_col, ROWS_BITS)
    earlier = lax.broadcasted_iota(jnp.int32, (tokens, tokens), 0) < lax.broadcasted_iota(
        jnp.int32, (tokens, tokens), 1)
    rank = jnp.sum(
        jnp.where(jnp.logical_and(earlier, owner_col == owner_row), 1.0, 0.0), axis=0, keepdims=True)
    slot = owner_row * cap + rank.astype(jnp.int32)
    pick = jnp.where(
        lax.broadcasted_iota(jnp.int32, (slots, tokens), 0) == slot, 1.0, 0.0).astype(BF16)
    number = idx_col - owner_col * ROWS_DEV + 1
    high = lax.shift_right_logical(number, 8)
    low = number - high * 256
    lane = lax.broadcasted_iota(jnp.int32, (tokens, LANES), 1)
    tags = jnp.where(lane == 0, high.astype(F32), jnp.where(lane == 1, low.astype(F32), 0.0))
    one = value.astype(BF16).astype(F32)
    two = (value - one).astype(BF16).astype(F32)
    three = value - one - two
    place = lax.broadcasted_iota(jnp.int32, value.shape, 1)
    share = jnp.where(place == 2, one, jnp.where(place == 3, two, jnp.where(place == 4, three, 0.0)))
    if cap > share.shape[0]:
        share = jnp.concatenate([share, jnp.zeros((cap - share.shape[0], LANES), F32)], axis=0)
    tagged = mm(pick, tags.astype(BF16)).reshape(slots // cap, cap, LANES) + share[None]
    return pick, tagged.reshape(slots, LANES).astype(BF16)


def back(late, beside, er, u, x, b, dxl, tail, db, dc, carry, w_in, grads_out):
    carry_all = jnp.concatenate([carry[0], carry[1]], axis=1)
    tail_v = tail[...]
    dx = dxl[...] + STEP_SIZE * tail_v * mm(b[...], carry_all)
    dbv = db[...] + STEP_SIZE * mm_t((tail_v * x[...].astype(F32)).astype(BF16), carry_all)
    dproj = jnp.concatenate([dx.astype(BF16), dbv.astype(BF16), dc[...].astype(BF16)], axis=1)
    uv = u[...]
    depth = uv.shape[1]
    ready = 0
    for j in range(dproj.shape[1] // LANES):
        grads_out[ready:ready + depth, :] = t_mm(uv, dproj[:, cut(j)]).astype(BF16)
        late.begin(ready, ready + depth)
        ready += depth
    beside()
    du = mm_t(dproj, w_in[...]).astype(BF16)
    erv = er[...]
    width = erv.shape[1]
    for j in range(du.shape[1] // LANES):
        grads_out[ready:ready + width, :] = t_mm(erv, du[:, cut(j)]).astype(BF16)
        late.begin(ready, ready + width)
        ready += width
    return du


def unpack(gout_in, grads_in, arrived_in, out_up, out_in, out_out, grad_skip, out_table,
           gout, grads, arrived, grad_up, grad_in, grad_out, grad_table, in_sems, out_sems):
    pairs = ((gout_in, gout), (grads_in, grads), (arrived_in, arrived))
    ins = [pltpu.make_async_copy(src, dst, in_sems.at[n]) for n, (src, dst) in enumerate(pairs)]
    pairs = ((grad_out, out_out), (grad_in, out_in), (grad_up, out_up), (grad_table, out_table))
    outs = [pltpu.make_async_copy(src, dst, out_sems.at[n]) for n, (src, dst) in enumerate(pairs)]
    for copy in ins:
        copy.start()
    inner = grad_out.shape[0]
    ins[0].wait()
    for j in range(grad_out.shape[1] // LANES):
        grad_out[:, cut(j)] = gout[inner * j:inner * (j + 1), :].astype(F32)
    outs[0].start()
    width, depth = grad_up.shape
    ins[1].wait()
    for j in range(grad_in.shape[1] // LANES):
        grad_in[:, cut(j)] = grads[depth * j:depth * (j + 1), :].astype(F32)
    outs[1].start()
    base = depth * (grad_in.shape[1] // LANES)
    for j in range(depth // LANES):
        grad_up[:, cut(j)] = grads[base + width * j:base + width * (j + 1), :].astype(F32)
    outs[2].start()
    ins[2].wait()
    tags = arrived[:, width:].astype(F32)
    number = tags[:, 0:1] * 256.0 + tags[:, 1:2] - 1.0
    slots = tags.shape[0]
    row = lax.broadcasted_iota(jnp.int32, (slots, ROWS_DEV), 1).astype(F32)
    pick = jnp.where(row == number, 1.0, 0.0).astype(BF16)
    grad_table[...] = t_mm(pick, arrived[:, :width])
    outs[3].start()
    heads = grad_skip.shape[1]
    cap = TILE
    parts = jnp.sum(tags.reshape(slots // cap, cap, LANES), axis=0)[:heads]
    place = lax.broadcasted_iota(jnp.int32, parts.shape, 1)
    kept = jnp.where(jnp.logical_and(place >= 2, place <= 4), parts, 0.0)
    sums = jnp.sum(kept, axis=1, keepdims=True)
    same = lax.broadcasted_iota(jnp.int32, (heads, heads), 0) == lax.broadcasted_iota(
        jnp.int32, (heads, heads), 1)
    grad_skip[...] = jnp.sum(jnp.where(same, sums, 0.0), axis=0, keepdims=True)
    for copy in outs:
        copy.wait()


def bit_count(n):
    return n.bit_length() - 1


class Summing:
    def __init__(self, rows, batch_n, ctx_n):
        names = [("batch", i) for i in range(bit_count(batch_n))]
        names += [("ctx", i) for i in range(bit_count(ctx_n))]
        rest = names[1:]
        self.levels = len(names) - 1
        tiles = rows // (batch_n * ctx_n) // TILE
        self.streams = []
        self.ends = []
        base = 0
        recv = 0
        self.sems = 0
        for s in range(3):
            mine = (tiles + 2 - s) // 3
            if mine == 0:
                continue
            turn = rest[:3]
            turn = turn[s:] + turn[:s]
            groups = [names[:1], turn[:1], turn[1:2], turn[2:3] + rest[3:4]]
            groups += [[name] for name in rest[4:]]
            size = mine * TILE << len(names)
            plan = []
            part = size
            for group in groups:
                part //= 1 << len(group)
                others = (1 << len(group)) - 1
                plan.append((group, part, recv, self.sems))
                recv += part * others
                self.sems += 2 * others
            self.streams.append((base, plan))
            base += size
            self.ends.append((base, size))
        self.recv_rows = recv

    def scratch(self, rows):
        return [
            pltpu.VMEM((rows, LANES), BF16),
            pltpu.VMEM((self.recv_rows, LANES), BF16),
            pltpu.VMEM((rows, LANES), BF16),
            pltpu.SemaphoreType.DMA((self.sems,)),
            pltpu.SemaphoreType.DMA((self.sems,)),
        ]

    def bind(self, where, acc, recv, full, send_sem, recv_sem):
        self.acc, self.recv, self.full = acc, recv, full
        self.copies = []
        self.keeps = []
        for base, plan in self.streams:
            off = base
            down, up, keeps = [], [], []
            for group, part, slot, sem in plan:
                members = 1 << len(group)
                bits = [(where[axis] // (1 << bit)) % 2 for axis, bit in group]
                mine = sum(value * (1 << n) for n, value in enumerate(bits))
                keep = pl.multiple_of(off + mine * part, TILE)
                downs, ups = [], []
                for d in range(1, members):
                    member = (mine + d) % members
                    at = dict(where)
                    for n, (axis, bit) in enumerate(group):
                        at[axis] = at[axis] + ((member // (1 << n)) % 2 - bits[n]) * (1 << bit)
                    target = (at["batch"], at["ctx"])
                    away = pl.multiple_of(off + member * part, TILE)
                    n = sem + 2 * (d - 1)
                    downs.append(pltpu.make_async_remote_copy(
                        src_ref=acc.at[pl.ds(away, part)],
                        dst_ref=recv.at[pl.ds(slot + (d - 1) * part, part)],
                        send_sem=send_sem.at[n], recv_sem=recv_sem.at[n],
                        device_id=target, device_id_type=MESH))
                    ups.append(pltpu.make_async_remote_copy(
                        src_ref=full.at[pl.ds(keep, part)], dst_ref=full.at[pl.ds(keep, part)],
                        send_sem=send_sem.at[n + 1], recv_sem=recv_sem.at[n + 1],
                        device_id=target, device_id_type=MESH))
                down.append(downs)
                up.append(ups)
                keeps.append((keep, part, slot))
                off = keep
            self.copies.append((down, up))
            self.keeps.append(keeps)

    def begin(self, low, high):
        for (end, _), (down, _) in zip(self.ends, self.copies):
            if low < end <= high:
                for copy in down[0]:
                    copy.start()

    def step(self, k):
        last = self.levels - 1
        for s, (down, up) in enumerate(self.copies):
            if k <= last:
                keep, part, slot = self.keeps[s][k]
                total = self.acc[pl.ds(keep, part), :].astype(F32)
                for n, copy in enumerate(down[k]):
                    copy.wait()
                    total += self.recv[pl.ds(slot + n * part, part), :].astype(F32)
                if k < last:
                    self.acc[pl.ds(keep, part), :] = total.astype(BF16)
                else:
                    self.full[pl.ds(keep, part), :] = total.astype(BF16)
                following = down[k + 1] if k < last else up[last]
            else:
                n = 2 * self.levels - 1 - k
                for copy in up[n]:
                    copy.wait()
                following = up[n - 1] if n > 0 else []
            for copy in following:
                copy.start()

    @property
    def steps(self):
        return 2 * self.levels


def joined(ref):
    return jnp.concatenate([ref[n] for n in range(ref.shape[0])], axis=1)


def position():
    return {"batch": lax.axis_index("batch"), "ctx": lax.axis_index("ctx")}


def middle(early, late, cap, batch_n, ctx_n,
           er, idx, decay, hs, dout, w_up, w_in, w_out, skip,
           gout_out, grads_out, arrived_out,
           sums, amount, u, x, b, dxl, tail, db, dc, y_buf, dsk, pick_buf,
           e_acc, e_recv, e_full, e_send, e_got, l_acc, l_recv, l_full, l_send, l_got,
           other, other_amount, moving, entering, entering_other, carry, c_send, c_recv,
           rows, arrived, r_send, r_recv, own_sem, out_sems):
    where = position()
    batch, ctx = where["batch"], where["ctx"]
    me = batch * ctx_n + ctx
    count = batch_n * ctx_n
    pair, place = ctx // 2, ctx % 2
    pairs = ctx_n // 2
    entering[...] = jnp.zeros_like(entering)
    partner = (batch, ctx + 1 - 2 * place)
    earlier = (batch, jnp.maximum(ctx - 2, 0))
    barrier = pltpu.get_barrier_semaphore()

    def at(step):
        to = (me + step) % count
        return to, (to // ctx_n, to % ctx_n)

    def hello(step, _):
        pl.semaphore_signal(barrier, inc=1, device_id=at(step)[1], device_id_type=MESH)
        return 0

    lax.fori_loop(1, count, hello, 0)
    kept = front(er, decay, dout, w_up, w_in, w_out, u, x, b, tail, sums, amount)
    pl.semaphore_wait(barrier, count - 1)

    def send(src, dst, n, target):
        return pltpu.make_async_remote_copy(
            src_ref=src, dst_ref=dst, send_sem=c_send.at[n], recv_sem=c_recv.at[n],
            device_id=target, device_id_type=MESH)

    amounts = send(amount, other_amount, 0, partner)
    halves = send(sums.at[1 - place], other.at[1 - place], 1, partner)
    second = send(sums.at[1], other.at[1], 2, partner)
    hops = [send(moving.at[n], entering.at[n], 5 + n, earlier) for n in range(entering.shape[0])]
    span = entering.shape[2]
    cross = send(entering, entering_other, 4, partner)
    amounts.start()
    halves.start()

    early.bind(where, e_acc, e_recv, e_full, e_send, e_got)
    late.bind(where, l_acc, l_recv, l_full, l_send, l_got)
    within(kept, hs, dout, skip, w_out.shape[0], dxl, db, dc, e_acc, y_buf, dsk)
    early.begin(0, e_acc.shape[0])
    width = er.shape[1]
    pick, tags = route(cap, rows.shape[0], idx[...], dsk[...])
    pick_buf[...] = pick
    rows[:, width:] = tags
    amounts.wait()
    halves.wait()

    @pl.when(place == 1)
    def _():
        second.start()

    mine = sums[place].astype(F32)
    theirs = other[place].astype(F32)
    a_mine = amount[place][0:1]
    a_theirs = other_amount[place][0:1]
    is_first = place == 0
    whole = jnp.where(is_first, mine + a_mine * theirs, theirs + a_theirs * mine)
    a_whole = a_mine * a_theirs
    done = 0
    for h in range(pairs - 2, -1, -1):
        @pl.when(pair == h + 1)
        def _():
            for n, hop in enumerate(hops):
                if h + 1 < pairs - 1:
                    hop.wait_recv()
                piece = slice(n * span, (n + 1) * span)
                moving[n] = (whole[:, piece] + a_whole[:, piece] * entering[n].astype(F32)).astype(BF16)
                hop.start()

        if done < early.levels:
            early.step(done)
            done += 1

    @pl.when(pair == 0)
    def _():
        for hop in hops:
            hop.wait_recv()

    cross.start()
    early.step(done)
    done += 1
    cross.wait()

    @pl.when(place == 1)
    def _():
        second.wait_send()
        carry[1] = joined(entering)
        carry[0] = joined(entering_other)

    @pl.when(place == 0)
    def _():
        second.wait_recv()
        carry[0] = (other[0].astype(F32) + other_amount[0][0:1] * joined(entering).astype(F32)).astype(BF16)
        carry[1] = (other[1].astype(F32) + other_amount[1][0:1] * joined(entering_other).astype(F32)).astype(BF16)

    @pl.when(pair > 0)
    def _():
        for hop in hops:
            hop.wait_send()

    du = back(late, lambda: early.step(done), er, u, x, b, dxl, tail, db, dc, carry, w_in, l_acc)
    done += 1
    rows[:, :width] = mm(pick_buf[...], mm_t(du, w_up[...]).astype(BF16)).astype(BF16)
    own_rows = pl.ds(pl.multiple_of(me * cap, TILE), cap)
    own = pltpu.make_async_copy(rows.at[own_rows], arrived.at[own_rows], own_sem)
    own.start()

    def row_copy(step):
        to, target = at(step)
        return pltpu.make_async_remote_copy(
            src_ref=rows.at[pl.ds(pl.multiple_of(to * cap, TILE), cap)], dst_ref=arrived.at[own_rows],
            send_sem=r_send.at[step], recv_sem=r_recv.at[step],
            device_id=target, device_id_type=MESH)

    def launch(step, _):
        row_copy(step).start()
        return 0

    lax.fori_loop(1, count, launch, 0)
    gout_copy = pltpu.make_async_copy(e_full, gout_out, out_sems.at[0])
    grads_copy = pltpu.make_async_copy(l_full, grads_out, out_sems.at[1])
    rows_done = pltpu.make_async_copy(arrived, arrived_out, out_sems.at[2])
    for k in range(late.steps):
        late.step(k)
        if done < early.steps:
            early.step(done)
            done += 1
            if done == early.steps:
                gout_copy.start()

    def finish(step, _):
        row_copy(step).wait()
        return 0

    grads_copy.start()
    lax.fori_loop(1, count, finish, 0)
    own.wait()
    rows_done.start()
    gout_copy.wait()
    grads_copy.wait()
    rows_done.wait()


def local(event_rows, event_index, decay, saved_state, dout, w_up, w_in, w_out, skip):
    batch_n = lax.axis_size("batch")
    ctx_n = lax.axis_size("ctx")
    count = batch_n * ctx_n
    er = event_rows[0]
    tokens, width = er.shape
    inner, depth = w_out.shape
    proj = w_in.shape[1]
    state = (proj - inner) // 2
    heads = skip.shape[0]
    half = inner // 2
    cap = TILE
    shape = jax.ShapeDtypeStruct
    params = pltpu.CompilerParams(vmem_limit_bytes=LIMIT)
    gout_rows = inner * depth // LANES
    grad_rows = (width * depth + depth * proj) // LANES
    slots = count * cap
    held = jnp.swapaxes(saved_state[0, 0], 1, 2).reshape(inner, state)
    early = Summing(gout_rows, batch_n, ctx_n)
    late = Summing(grad_rows, batch_n, ctx_n)
    gout, grads, arrived = pl.pallas_call(
        partial(middle, early, late, cap, batch_n, ctx_n),
        out_shape=(
            shape((gout_rows, LANES), BF16), shape((grad_rows, LANES), BF16),
            shape((slots, width + LANES), BF16),
        ),
        in_specs=[VMEM] * 8 + [SMEM],
        out_specs=[pl.BlockSpec(memory_space=pl.ANY)] * 3,
        scratch_shapes=[
            pltpu.VMEM((2, state, half), BF16),
            pltpu.VMEM((2, 8, half), F32),
            pltpu.VMEM((tokens, depth), BF16),
            pltpu.VMEM((tokens, inner), BF16),
            pltpu.VMEM((tokens, state), BF16),
            pltpu.VMEM((tokens, inner), F32),
            pltpu.VMEM((tokens, inner), F32),
            pltpu.VMEM((tokens, state), F32),
            pltpu.VMEM((tokens, state), F32),
            pltpu.VMEM((tokens, inner), BF16),
            pltpu.VMEM((heads, LANES), F32),
            pltpu.VMEM((slots, tokens), BF16),
        ] + early.scratch(gout_rows) + late.scratch(grad_rows) + [
            pltpu.VMEM((2, state, half), BF16),
            pltpu.VMEM((2, 8, half), F32),
            pltpu.VMEM((2, state, half // 2), BF16),
            pltpu.VMEM((2, state, half // 2), BF16),
            pltpu.VMEM((2, state, half // 2), BF16),
            pltpu.VMEM((2, state, half), BF16),
            pltpu.SemaphoreType.DMA((7,)),
            pltpu.SemaphoreType.DMA((7,)),
            pltpu.VMEM((slots, width + LANES), BF16),
            pltpu.VMEM((slots, width + LANES), BF16),
            pltpu.SemaphoreType.DMA((count,)),
            pltpu.SemaphoreType.DMA((count,)),
            pltpu.SemaphoreType.DMA,
            pltpu.SemaphoreType.DMA((3,)),
        ],
        compiler_params=pltpu.CompilerParams(
            vmem_limit_bytes=LIMIT, collective_id=0, has_side_effects=True),
        name="middle",
    )(er, event_index, decay[0], held, dout[0], w_up, w_in, w_out, skip)

    grad_up, grad_in, grad_out, grad_skip, grad_table = pl.pallas_call(
        unpack,
        out_shape=(
            shape((width, depth), F32), shape((depth, proj), F32), shape((inner, depth), F32),
            shape((1, heads), F32), shape((ROWS_DEV, width), F32),
        ),
        in_specs=[pl.BlockSpec(memory_space=pl.ANY)] * 3,
        out_specs=[pl.BlockSpec(memory_space=pl.ANY)] * 3 + [VMEM, pl.BlockSpec(memory_space=pl.ANY)],
        scratch_shapes=[
            pltpu.VMEM(gout.shape, BF16),
            pltpu.VMEM(grads.shape, BF16),
            pltpu.VMEM(arrived.shape, BF16),
            pltpu.VMEM((width, depth), F32),
            pltpu.VMEM((depth, proj), F32),
            pltpu.VMEM((inner, depth), F32),
            pltpu.VMEM((ROWS_DEV, width), F32),
            pltpu.SemaphoreType.DMA((3,)),
            pltpu.SemaphoreType.DMA((4,)),
        ],
        compiler_params=params,
        name="unpack",
    )(gout, grads, arrived)
    return grad_up, grad_in, grad_out, grad_skip[0], grad_table


def solution(mesh):
    in_specs = (
        P("batch", "ctx", None),
        P("batch", "ctx"),
        P("batch", None, "ctx"),
        P("batch", "ctx", None, None, None),
        P("batch", "ctx", None),
        P(),
        P(),
        P(),
        P(),
    )
    out_specs = (P(), P(), P(), P(), P(("batch", "ctx"), None))
    return jax.shard_map(local, mesh=mesh, in_specs=in_specs, out_specs=out_specs, check_vma=False)
```
